256 devices in a mesh: img: 8 (over z), cls: 32 (over x, y, core).
Axes of the slice: x: 4, y: 4, z: 8, core: 2. Of those that a mesh axis runs over, the one named last changes fastest.
Arguments:
- picture_token_states: bfloat16 [8192, 1664], P(('img', 'cls')), may hold values from -6 to 90
- layer_scaling_coefficients: float32 [1664], replicated, may hold values from 0.5 to 1.5
- expanding_linear_map: bfloat16 [1664, 8192], P(None, 'cls'), may hold values from -0.15625 to 0.15625
- contracting_linear_map: bfloat16 [8192, 1664], P('cls'), may hold values from -0.0625 to 0.0625
- closing_scaling_coefficients: float32 [1664], replicated, may hold values from 0.5 to 1.5
- joint_space_mapper: bfloat16 [1664, 1280], replicated, may hold values from -0.0501 to 0.0501
- prompt_caption_encodings: bfloat16 [16384, 16, 1280], P('cls', 'img'), may hold values from -6 to 6
- prompt_category_multiplicity: int32 [16384, 16], P('cls'), may hold values from 1 to 9
- sharpness_multiplier: float32 [1], replicated, may hold values from 280 to 420
Outputs:
- log_probs: float32 [8192, 16384], P('img', 'cls')
The draws below stay inside these ranges and needn't reach their ends.
All inputs are finite; a program needn't handle non-finite values.
Results may differ from the reference program's by a relative error of at most 0.0059.
Values may be sent and summed in bfloat16 or wider, within the bound.
A program may use at most 64 MiB of HBM per device.

```python
import math
import jax
import jax.numpy as jnp
from jax import lax

D = 1664
FF = 8192
E = 1280
TPL_DEV = 2
IMAGES = 8192
CLASSES = 16384
TEMPL = 16
N_IMG = 8
N_CLS = 32


concept_count = 8


def shared_parts(key):
    feature_key, class_key, weight_key = jax.random.split(key, 3)
    features = jax.random.permutation(feature_key, D)[:concept_count].astype(jnp.int32)
    chosen = jax.random.permutation(class_key, CLASSES)[:2 * concept_count].astype(jnp.int32)
    weights = jax.random.uniform(weight_key, (D, E), jnp.float32, -0.05, 0.05)
    return (features, chosen, weights)


def draw_joint_space_mapper(key, part):
    features, chosen, weights = shared_parts(key)
    return weights.astype(jnp.bfloat16)


def draw_picture_token_states(key, part):
    features, chosen, weights = shared_parts(key)
    key = jax.random.fold_in(key, 5)
    noise_key, pick_key, concept_key = jax.random.split(key, 3)
    noise = jnp.clip(jax.random.normal(noise_key, (IMAGES, D), jnp.float32), -6.0, 6.0)
    picked = jax.random.randint(pick_key, (IMAGES,), 0, 4) == 0
    concept = jax.random.randint(concept_key, (IMAGES,), 0, concept_count)
    strength = 90.0 * (4 + concept).astype(jnp.float32) / 11.0
    column = features[concept]
    spike = picked[:, None] & (jnp.arange(D)[None, :] == column[:, None])
    values = jnp.where(spike, strength[:, None], noise)
    return values.astype(jnp.bfloat16)


def draw_prompt_caption_encodings(key, part):
    features, chosen, weights = shared_parts(key)
    key = jax.random.fold_in(key, 7)
    first_key, second_key = jax.random.split(key)
    base = jax.random.normal(first_key, (CLASSES, 1, E), jnp.float32)
    noise = jax.random.normal(second_key, (CLASSES, TEMPL, E), jnp.float32)
    direction = weights[features] * (1.7320508 / 0.05)
    paired = jnp.repeat(direction, 2, axis=0)
    match = jnp.arange(CLASSES)[:, None] == chosen[None, :]
    slot = jnp.sum(jnp.where(match, jnp.arange(2 * concept_count)[None, :], 0), axis=1)
    hit = jnp.any(match, axis=1)
    aligned = paired[slot]
    amplitude = jnp.where(slot % 2 == 0, 0.2, 0.235)
    values = jnp.where(hit[:, None, None], aligned[:, None, :] + amplitude[:, None, None] * noise, base + 0.6 * noise)
    values = jnp.clip(values, -6.0, 6.0)
    return values.astype(jnp.bfloat16)


def touch_ends(array, stream_key, low, high):
    longest = array.shape.index(max(array.shape))
    spots = []
    for shift in (0, 1):
        where = [jax.random.randint(jax.random.fold_in(stream_key, axis), (), 0, length) for axis, length in enumerate(array.shape)]
        where[longest] = (where[longest] + shift) % array.shape[longest]
        spots.append(tuple(where))
    return array.at[spots[0]].set(low).at[spots[1]].set(high)


def block_levels(rng, extent, shards, smallest, high):
    level = 1.0
    for dim, blocks in shards:
        heights = jax.random.uniform(jax.random.fold_in(jax.random.fold_in(rng, 6), dim), (blocks,), jnp.float32, smallest / len(shards), high / len(shards))
        level = level * jnp.repeat(jnp.exp(heights), extent[dim] // blocks).reshape((-1,) + (1,) * (len(extent) - 1 - dim))
    return level


def bell_draw(stream_key, dims, deviation, most, cuts=(), dtype=jnp.bfloat16):
    drawn = deviation * jax.random.normal(stream_key, dims, jnp.float32)
    if cuts:
        drawn = drawn * block_levels(stream_key, dims, cuts, -0.22, 0.18)
    return jnp.clip(drawn, -most, most).astype(dtype)


def setup_inputs(seed: int = 0) -> dict:
    seeds = jax.random.split(jax.random.key(seed), 10)
    picture_token_states = draw_picture_token_states(jax.random.fold_in(seeds[9], 71), 0)
    layer_scaling_coefficients = jnp.clip(1.0 + 0.1 * jax.random.normal(seeds[1], (D,), jnp.float32), 0.5, 1.5)
    expanding_linear_map = bell_draw(seeds[2], (D, FF), D ** -0.5, 0.15625, ((1, 32),))
    contracting_linear_map = bell_draw(seeds[3], (FF, D), FF ** -0.5, 0.0625, ((0, 32),))
    closing_scaling_coefficients = jnp.clip(1.0 + 0.1 * jax.random.normal(seeds[4], (D,), jnp.float32), 0.5, 1.5)
    joint_space_mapper = draw_joint_space_mapper(jax.random.fold_in(seeds[9], 71), 0)
    prompt_caption_encodings = draw_prompt_caption_encodings(jax.random.fold_in(seeds[9], 71), 0)
    prompt_category_multiplicity = touch_ends(jax.random.randint(seeds[7], (CLASSES, TEMPL), 1, 10), jax.random.fold_in(seeds[7], 1), 1, 9).astype(jnp.int32)
    sharpness_multiplier = jnp.clip(jnp.exp(jax.random.uniform(seeds[8], (1,), jnp.float32, math.log(280.0), math.log(420.0))), 280.0, 420.0)
    return dict(picture_token_states=picture_token_states, layer_scaling_coefficients=layer_scaling_coefficients, expanding_linear_map=expanding_linear_map, contracting_linear_map=contracting_linear_map, closing_scaling_coefficients=closing_scaling_coefficients, joint_space_mapper=joint_space_mapper, prompt_caption_encodings=prompt_caption_encodings, prompt_category_multiplicity=prompt_category_multiplicity, sharpness_multiplier=sharpness_multiplier)


epsilon = 1e-05

def layer_norm(values, gain_vec):
    center = values - lax.optimization_barrier(jnp.mean(values, axis=-1, keepdims=True))
    variance = lax.optimization_barrier(jnp.mean(center * center, axis=-1, keepdims=True))
    return center * lax.rsqrt(variance + epsilon) * gain_vec

def reference(picture_token_states, layer_scaling_coefficients, expanding_linear_map, contracting_linear_map, closing_scaling_coefficients, joint_space_mapper, prompt_caption_encodings, prompt_category_multiplicity, sharpness_multiplier):
    residual = picture_token_states.astype(jnp.float32)
    normed = layer_norm(residual, layer_scaling_coefficients).astype(jnp.bfloat16)
    hidden = jax.nn.gelu(jnp.dot(normed, expanding_linear_map, preferred_element_type=jnp.float32), approximate=False).astype(jnp.bfloat16)
    block_width = FF // N_CLS
    stream = residual
    for block_index in range(N_CLS):
        lower = block_index * block_width
        upper = lower + block_width
        block_term = jnp.dot(hidden[:, lower:upper], contracting_linear_map[lower:upper], preferred_element_type=jnp.float32).astype(jnp.bfloat16)
        stream = stream + lax.optimization_barrier(block_term).astype(jnp.float32)
    pooled = layer_norm(stream, closing_scaling_coefficients).astype(jnp.bfloat16)
    projected = jnp.dot(pooled, joint_space_mapper, preferred_element_type=jnp.float32)
    joint_space_features = (projected * lax.rsqrt(lax.optimization_barrier(jnp.sum(projected * projected, axis=-1, keepdims=True)) + 1e-06)).astype(jnp.bfloat16)
    weights_f = prompt_category_multiplicity.astype(jnp.float32)
    share = weights_f / lax.optimization_barrier(jnp.sum(weights_f, axis=1, keepdims=True))
    blended = jnp.zeros((CLASSES, E), jnp.float32)
    for group in range(N_IMG):
        tmpl = prompt_caption_encodings[:, group * TPL_DEV:(group + 1) * TPL_DEV].astype(jnp.float32)
        unit_templates = tmpl * lax.rsqrt(lax.optimization_barrier(jnp.sum(tmpl * tmpl, axis=-1, keepdims=True)) + 1e-06)
        group_sum = jnp.einsum('ct,cte->ce', share[:, group * TPL_DEV:(group + 1) * TPL_DEV], unit_templates).astype(jnp.bfloat16)
        blended = blended + lax.optimization_barrier(group_sum).astype(jnp.float32)
    category_prototype_array = blended.astype(jnp.bfloat16)
    category_affinity_values = lax.dot_general(joint_space_features, category_prototype_array, (((1,), (1,)), ((), ())), preferred_element_type=jnp.float32) * sharpness_multiplier[0]
    row_max = lax.optimization_barrier(jnp.max(category_affinity_values, axis=1, keepdims=True))
    row_total = lax.optimization_barrier(jnp.sum(jnp.exp(category_affinity_values - row_max), axis=1, keepdims=True))
    return category_affinity_values - row_max - jnp.log(row_total)
```

```python
import jax
import jax.numpy as jnp
from jax import lax
from jax.experimental import pallas as pl
from jax.experimental.pallas import tpu as pltpu
from jax.sharding import PartitionSpec as P

MESH = pl.DeviceIdType.MESH
F32 = jnp.float32
BF16 = jnp.bfloat16
ORDER = (1, 3, 2)


def layer_norm(values, gain):
    center = values - jnp.mean(values, axis=-1, keepdims=True)
    variance = jnp.mean(center * center, axis=-1, keepdims=True)
    return center * lax.rsqrt(variance + 1e-05) * gain


def arrived(ref, sem):
    pltpu.make_async_copy(ref, ref, sem).wait()


class PlaneGather:
    def __init__(self, x, y, at, buf, sems):
        self.x, self.y, self.at, self.buf = x, y, at, buf
        self.a1, self.a2, self.b1, self.b2, self.out = sems

    def send(self, h, xx, yy, to, sem):
        piece = self.buf.at[h, xx * 4 + yy]
        pltpu.make_async_remote_copy(
            src_ref=piece, dst_ref=piece, send_sem=self.out, recv_sem=sem, device_id=to, device_id_type=MESH
        ).start()

    def start(self):
        x, y = self.x, self.y
        for d in ORDER:
            self.send(0, x, y, self.at((x + d) % 4, y), self.a1.at[4 - d])
            self.send(1, x, y, self.at(x, (y + d) % 4), self.b1.at[4 - d])
        for d in ORDER:
            self.send(0, x, y, self.at(x, (y + d) % 4), self.a2.at[0])
            self.send(1, x, y, self.at((x + d) % 4, y), self.b2.at[4 - d])

    def forward(self):
        x, y = self.x, self.y
        for o in ORDER:
            xs, ys = (x + o) % 4, (y + o) % 4
            arrived(self.buf.at[0, xs * 4 + y], self.a1.at[o])
            for d in ORDER:
                self.send(0, xs, y, self.at(x, (y + d) % 4), self.a2.at[o])
            arrived(self.buf.at[1, x * 4 + ys], self.b1.at[o])
            for d in ORDER:
                self.send(1, x, ys, self.at((x + d) % 4, y), self.b2.at[4 - d])

    def column(self, o):
        arrived(self.buf.at[0, pl.ds(0, 3)], self.a2.at[o])
        if o:
            arrived(self.buf.at[1, pl.ds(0, 4)], self.b2.at[o])

    def finish(self):
        arrived(self.buf.at[:, pl.ds(0, 15)], self.out)


def kernel(
    x_ref, g1_ref, w1_hbm, w2_hbm, g2_ref, map_hbm, tpl_hbm, mult_ref, sharp_ref,
    logit_out, lse_out,
    tok, w1, w2, part, r1a, r1b, s1a, s1b, r2a, r2b, mapv, emb, tplv, shc, gs, zr, zs, cls, lg, lse_mine, lse_in,
    load_sem, w_send, w_recv, g_a1, g_a2, g_b1, g_b2, g_out, e_a1, e_a2, e_b1, e_b2, e_out,
    ra1, rb1, ra2, rb2, rs_out, z_recv, z_out, za_recv, za_out, pair_recv, pair_out, lo_sem, l_recv, l_out,
):
    m = lax.axis_index("cls")
    z = lax.axis_index("img")
    x, y, c = m // 8, (m // 2) % 4, m % 2
    me = x * 4 + y

    def at(xx, yy):
        return (z, (xx * 4 + yy) * 2 + c)

    mate = (z, me * 2 + (1 - c))
    z_up, z_down = ((z + 1) % 8, m), ((z + 7) % 8, m)

    def send(src, dst, s_sem, r_sem, to):
        pltpu.make_async_remote_copy(
            src_ref=src, dst_ref=dst, send_sem=s_sem, recv_sem=r_sem, device_id=to, device_id_type=MESH
        ).start()

    barrier = pltpu.get_barrier_semaphore()
    partners = [at((x + d) % 4, y) for d in ORDER] + [at(x, (y + d) % 4) for d in ORDER] + [mate, z_up, z_down]
    for to in partners:
        pl.semaphore_signal(barrier, inc=1, device_id=to, device_id_type=MESH)

    loads = [
        pltpu.make_async_copy(tpl_hbm, tplv, load_sem.at[0]),
        pltpu.make_async_copy(w1_hbm, w1.at[c], load_sem.at[1]),
        pltpu.make_async_copy(w2_hbm, w2.at[c], load_sem.at[2]),
        pltpu.make_async_copy(map_hbm, mapv, load_sem.at[3]),
    ]
    for load in loads:
        load.start()

    states = x_ref[...].astype(F32)
    normed = layer_norm(states, g1_ref[...][None, :]).astype(BF16)
    tok[0, me] = normed[:16]
    tok[1, me] = normed[16:]

    pl.semaphore_wait(barrier, len(partners))

    gather = PlaneGather(x, y, at, tok, (g_a1, g_a2, g_b1, g_b2, g_out))
    gather.start()
    send(w1_hbm, w1.at[c], w_send.at[0], w_recv.at[0], mate)
    send(w2_hbm, w2.at[c], w_send.at[1], w_recv.at[1], mate)

    weights = mult_ref[...].astype(F32)
    total = jnp.sum(weights, axis=0, keepdims=True)
    row_id = lax.broadcasted_iota(jnp.int32, weights.shape, 0)
    for t in range(2):
        own = jnp.sum(jnp.where(row_id == 2 * z + t, weights, 0.0), axis=0, keepdims=True)
        portion = own / total
        for q in range(4):
            shc[t, pl.ds(q * 128, 128), :] = jnp.broadcast_to(portion[:, q * 128 : (q + 1) * 128], (128, 128)).T

    def group_sums(lo, hi):
        @pl.loop(lo, hi)
        def _(k):
            for i in range(2):
                rows = pl.ds(k * 64 + i * 32, 32)
                acc = None
                for t in range(2):
                    tmpl = tplv[t, rows, :].astype(F32)
                    coef = shc[t, rows, 0:1] * lax.rsqrt(jnp.sum(tmpl * tmpl, axis=-1, keepdims=True) + 1e-06)
                    acc = coef * tmpl if acc is None else acc + coef * tmpl
                gs[k, pl.ds(i * 32, 32), :] = acc.astype(BF16)

    loads[0].wait()
    group_sums(0, 4)
    gather.forward()
    group_sums(4, 8)

    halves = (pl.ds(0, 640), pl.ds(640, 640))

    def z_reduce(s):
        for way, half in ((0, 0), (1, 1), (0, 1), (1, 0)):
            if s == 0 and way != half:
                continue
            cols = halves[half]
            k = (z + 4 + s) % 8 if way == 0 else (z + 4 - s + 8) % 8
            first = s == 0 or (s == 1 and way != half)
            if first:
                src = gs.at[k, :, cols]
            else:
                came = zr.at[way, s - 1, :, cols]
                arrived(came, z_recv.at[way, half, s - 1])
                zs[way, s, :, cols] = (gs[k, :, cols].astype(F32) + came[...].astype(F32)).astype(BF16)
                src = zs.at[way, s, :, cols]
            send(src, zr.at[way, s, :, cols], z_out, z_recv.at[way, half, s], z_down if way == 0 else z_up)

    def z_total():
        for half in range(2):
            cols = halves[half]
            for way in range(2):
                arrived(zr.at[way, 3, :, cols], z_recv.at[way, half, 3])
            cls[z, :, cols] = (
                gs[z, :, cols].astype(F32) + zr[0, 3, :, cols].astype(F32) + zr[1, 3, :, cols].astype(F32)
            ).astype(BF16)

    def z_gather(s):
        for way, half in ((0, 0), (1, 1), (0, 1), (1, 0)):
            cols = halves[half]
            far = 4 if way == half else 3
            k = (z + s) % 8 if way == 0 else (z - s + 8) % 8
            if s > far:
                continue
            chunk = cls.at[k, :, cols]
            if s > 0:
                arrived(chunk, za_recv.at[way, half, s - 1])
            if s < far:
                send(chunk, chunk, za_out, za_recv.at[way, half, s], z_down if way == 0 else z_up)

    z_reduce(0)

    def ffn(o):
        xs = (x + o) % 4
        gather.column(o)
        rows = tok[:, pl.ds(xs * 4, 4)].reshape(128, tok.shape[-1])
        out = None
        for k in range(2):
            pre = jnp.dot(rows, w1[k], preferred_element_type=F32)
            hidden = (pre * 0.5 * (1.0 + lax.erf(pre * 0.7071067811865476))).astype(BF16)
            term = jnp.dot(hidden, w2[k], preferred_element_type=F32)
            out = term if out is None else out + term
        part[:, pl.ds(xs * 4, 4)] = out.astype(BF16).reshape(2, 4, 16, tok.shape[-1])
        for d in ORDER:
            yd = (y + d) % 4
            send(part.at[0, xs * 4 + yd], r1a.at[3 - d, o], rs_out.at[0], ra1.at[o], at(x, yd))
        if o:
            send(part.at[1, pl.ds(xs * 4, 4)], r1b.at[3 - o], rs_out.at[1], rb1.at[3 - o], at(xs, y))

    loads[1].wait()
    loads[2].wait()
    arrived(w1.at[1 - c], w_recv.at[0])
    arrived(w2.at[1 - c], w_recv.at[1])
    ffn(0)
    z_reduce(1)
    ffn(1)
    ffn(3)
    z_reduce(2)
    ffn(2)

    for o in ORDER:
        xs = (x + o) % 4
        arrived(r1a.at[:, o], ra1.at[o])
        s1a[o] = (
            part[0, xs * 4 + y].astype(F32) + r1a[0, o].astype(F32) + r1a[1, o].astype(F32) + r1a[2, o].astype(F32)
        ).astype(BF16)
        send(s1a.at[o], r2a.at[3 - o], rs_out.at[2], ra2.at[0], at(xs, y))
    z_reduce(3)
    for k in range(3):
        arrived(r1b.at[k], rb1.at[k])
    for o in ORDER:
        ys = (y + o) % 4
        s1b[o] = (
            part[1, x * 4 + ys].astype(F32) + r1b[0, ys].astype(F32) + r1b[1, ys].astype(F32) + r1b[2, ys].astype(F32)
        ).astype(BF16)
        send(s1b.at[o], r2b.at[3 - o], rs_out.at[3], rb2.at[0], at(x, ys))
    arrived(r1a.at[:, 0], ra1.at[0])
    own_a = part[0, me].astype(F32) + r1a[0, 0].astype(F32) + r1a[1, 0].astype(F32) + r1a[2, 0].astype(F32)
    own_b = part[1, me].astype(F32) + r1b[0, y].astype(F32) + r1b[1, y].astype(F32) + r1b[2, y].astype(F32)
    gather.finish()
    arrived(r2a, ra2.at[0])
    arrived(r2b, rb2.at[0])
    for k in range(3):
        own_a = own_a + r2a[k].astype(F32)
        own_b = own_b + r2b[k].astype(F32)
    stream = states + jnp.concatenate([own_a, own_b], axis=0)
    pooled = layer_norm(stream, g2_ref[...][None, :]).astype(BF16)
    loads[3].wait()
    projected = jnp.dot(pooled, mapv[...], preferred_element_type=F32)
    embedding = (
        projected * lax.rsqrt(jnp.sum(projected * projected, axis=-1, keepdims=True) + 1e-06)
    ).astype(BF16)
    emb[c, 0, me] = embedding[:16]
    emb[c, 1, me] = embedding[16:]
    spread = PlaneGather(x, y, at, emb.at[c], (e_a1, e_a2, e_b1, e_b2, e_out))
    spread.start()
    z_total()
    z_gather(0)
    spread.forward()
    z_gather(1)
    z_gather(2)
    z_gather(3)
    z_gather(4)

    sharp = sharp_ref[0]

    def logits(core, o):
        xs = (x + o) % 4
        rows = emb[core, :, pl.ds(xs * 4, 4)].reshape(128, emb.shape[-1])
        classes = cls[...].reshape(512, emb.shape[-1])
        val = sharp * lax.dot_general(rows, classes, (((1,), (1,)), ((), ())), preferred_element_type=F32)
        for h in range(2):
            for yy in range(4):
                lo = h * 64 + yy * 16
                lg[xs * 4 + yy, core, h] = val[lo : lo + 16]
        pltpu.make_async_copy(lg.at[pl.ds(xs * 4, 4), core], logit_out.at[pl.ds(xs * 4, 4), core], lo_sem).start()
        top = jnp.max(val, axis=-1, keepdims=True)
        lse = top + jnp.log(jnp.sum(jnp.exp(val - top), axis=-1, keepdims=True))
        lse_mine[0, pl.ds(core * 4 + xs, 1), :] = jnp.broadcast_to(lse, (128, 128)).T[0:1, :]

    def own_column(o):
        spread.column(o)
        quad = emb.at[c, :, pl.ds(((x + o) % 4) * 4, 4)]
        send(quad, quad, pair_out, pair_recv.at[o], mate)

    def mate_column(o):
        arrived(emb.at[1 - c, :, pl.ds(((x + o) % 4) * 4, 4)], pair_recv.at[o])

    own_column(0)
    logits(c, 0)
    own_column(1)
    logits(c, 1)
    mate_column(0)
    logits(1 - c, 0)
    own_column(3)
    logits(c, 3)
    mate_column(1)
    logits(1 - c, 1)
    own_column(2)
    logits(c, 2)
    mate_column(3)
    logits(1 - c, 3)
    mate_column(2)
    logits(1 - c, 2)

    def merge(values):
        top = values[0]
        for v in values[1:]:
            top = jnp.maximum(top, v)
        acc = jnp.exp(values[0] - top)
        for v in values[1:]:
            acc = acc + jnp.exp(v - top)
        return top + jnp.log(acc)

    send(lse_mine.at[0], lse_in.at[0], l_out.at[0], l_recv.at[0], mate)
    arrived(lse_in.at[0], l_recv.at[0])
    lse_mine[1] = merge([lse_mine[0], lse_in[0]])
    for d in ORDER:
        send(lse_mine.at[1], lse_in.at[4 - d], l_out.at[1], l_recv.at[4 - d], at((x + d) % 4, y))
    for d in ORDER:
        arrived(lse_in.at[d], l_recv.at[d])
    lse_mine[2] = merge([lse_mine[1]] + [lse_in[d] for d in ORDER])
    for d in ORDER:
        send(lse_mine.at[2], lse_in.at[3 + 4 - d], l_out.at[2], l_recv.at[3 + 4 - d], at(x, (y + d) % 4))

    spread.finish()
    arrived(w1.at[c], w_send.at[0])
    arrived(w2.at[c], w_send.at[1])
    arrived(part.at[0, pl.ds(0, 12)], rs_out.at[0])
    arrived(part.at[0, pl.ds(0, 12)], rs_out.at[1])
    arrived(r2a, rs_out.at[2])
    arrived(r2b, rs_out.at[3])
    arrived(gs.at[pl.ds(0, 7)], z_out)
    arrived(gs.at[pl.ds(0, 7)], za_out)
    arrived(emb.at[c], pair_out)
    arrived(lg, lo_sem)
    arrived(lse_in.at[0], l_out.at[0])
    arrived(lse_in.at[pl.ds(0, 3)], l_out.at[1])

    for d in ORDER:
        arrived(lse_in.at[3 + d], l_recv.at[3 + d])
    lse = merge([lse_mine[2]] + [lse_in[3 + d] for d in ORDER])
    for q in range(8):
        columns = jnp.broadcast_to(lse[q : q + 1, :], (128, 128)).T
        for h in range(2):
            for yy in range(4):
                lo = h * 64 + yy * 16
                lse_out[(q % 4) * 4 + yy, q // 4, h] = columns[lo : lo + 16]
    arrived(lse_in.at[pl.ds(0, 3)], l_out.at[2])


def shards(states, gain1, w1, w2, gain2, mapper, prompts, multiplicity, sharpness):
    width = states.shape[1]
    edim = mapper.shape[1]
    vmem = pl.BlockSpec(memory_space=pltpu.VMEM)
    anywhere = pl.BlockSpec(memory_space=pl.ANY)
    dma = pltpu.SemaphoreType.DMA
    logit, lse = pl.pallas_call(
        kernel,
        name="whole",
        out_shape=(
            jax.ShapeDtypeStruct((16, 2, 2, 16, 512), F32),
            jax.ShapeDtypeStruct((16, 2, 2, 16, 128), F32),
        ),
        in_specs=[vmem, vmem, anywhere, anywhere, vmem, anywhere, anywhere, vmem, pl.BlockSpec(memory_space=pltpu.SMEM)],
        out_specs=(anywhere, vmem),
        scratch_shapes=[
            pltpu.VMEM((2, 16, 16, width), BF16),
            pltpu.VMEM((2, width, 256), BF16),
            pltpu.VMEM((2, 256, width), BF16),
            pltpu.VMEM((2, 16, 16, width), BF16),
            pltpu.VMEM((3, 4, 16, width), BF16),
            pltpu.VMEM((3, 4, 16, width), BF16),
            pltpu.VMEM((4, 16, width), BF16),
            pltpu.VMEM((4, 16, width), BF16),
            pltpu.VMEM((3, 16, width), BF16),
            pltpu.VMEM((3, 16, width), BF16),
            pltpu.VMEM((width, edim), BF16),
            pltpu.VMEM((2, 2, 16, 16, edim), BF16),
            pltpu.VMEM((2, 512, edim), BF16),
            pltpu.VMEM((2, 512, 128), F32),
            pltpu.VMEM((8, 64, edim), BF16),
            pltpu.VMEM((2, 4, 64, edim), BF16),
            pltpu.VMEM((2, 4, 64, edim), BF16),
            pltpu.VMEM((8, 64, edim), BF16),
            pltpu.VMEM((16, 2, 2, 16, 512), F32),
            pltpu.VMEM((3, 8, 128), F32),
            pltpu.VMEM((7, 8, 128), F32),
            dma((4,)), dma((2,)), dma((2,)),
            dma((4,)), dma((4,)), dma((4,)), dma((4,)), dma(()),
            dma((4,)), dma((4,)), dma((4,)), dma((4,)), dma(()),
            dma((4,)), dma((3,)), dma((1,)), dma((1,)), dma((4,)),
            dma((2, 2, 4)), dma(()), dma((2, 2, 4)), dma(()),
            dma((4,)), dma(()), dma(()),
            dma((7,)), dma((3,)),
        ],
        compiler_params=pltpu.CompilerParams(
            collective_id=0, has_side_effects=True, vmem_limit_bytes=50 * 1024 * 1024
        ),
    )(states, gain1, w1, w2, gain2, mapper, jnp.transpose(prompts, (1, 0, 2)), multiplicity.T, sharpness)
    return logit.reshape(1024, 512) - lse.reshape(1024, 128)[:, :1]


def solution(mesh):
    in_specs = (
        P(("img", "cls"), None),
        P(),
        P(None, "cls"),
        P("cls", None),
        P(),
        P(),
        P("cls", "img", None),
        P("cls", None),
        P(),
    )
    out_specs = P("img", "cls")
    return jax.shard_map(shards, mesh=mesh, in_specs=in_specs, out_specs=out_specs, check_vma=False)
```

```python
import jax
import jax.numpy as jnp
from jax import lax
from jax.experimental import pallas as pl
from jax.experimental.pallas import tpu as pltpu
from jax.sharding import PartitionSpec as P

MESH = pl.DeviceIdType.MESH
F32 = jnp.float32
BF16 = jnp.bfloat16
ORDER = (1, 3, 2)


def layer_norm(values, gain):
    center = values - jnp.mean(values, axis=-1, keepdims=True)
    variance = jnp.mean(center * center, axis=-1, keepdims=True)
    return center * lax.rsqrt(variance + 1e-05) * gain


def arrived(ref, sem):
    pltpu.make_async_copy(ref, ref, sem).wait()


class PlaneGather:
    def __init__(self, x, y, at, buf, split, sems):
        self.x, self.y, self.at, self.buf = x, y, at, buf
        self.cols = (pl.ds(0, split), pl.ds(split, buf.shape[-1] - split))
        self.a1, self.a2, self.b1, self.b2, self.out = sems

    def send(self, p, xx, yy, to, sem):
        piece = self.buf.at[xx * 4 + yy, :, self.cols[p]]
        pltpu.make_async_remote_copy(
            src_ref=piece, dst_ref=piece, send_sem=self.out, recv_sem=sem, device_id=to, device_id_type=MESH
        ).start()

    def start(self):
        x, y = self.x, self.y
        for d in ORDER:
            self.send(0, x, y, self.at((x + d) % 4, y), self.a1.at[4 - d])
            self.send(1, x, y, self.at(x, (y + d) % 4), self.b1.at[4 - d])
        for d in ORDER:
            self.send(0, x, y, self.at(x, (y + d) % 4), self.a2.at[0])
            self.send(1, x, y, self.at((x + d) % 4, y), self.b2.at[4 - d])

    def forward(self):
        x, y = self.x, self.y
        for o in ORDER:
            xs, ys = (x + o) % 4, (y + o) % 4
            arrived(self.buf.at[xs * 4 + y, :, self.cols[0]], self.a1.at[o])
            for d in ORDER:
                self.send(0, xs, y, self.at(x, (y + d) % 4), self.a2.at[o])
            arrived(self.buf.at[x * 4 + ys, :, self.cols[1]], self.b1.at[o])
            for d in ORDER:
                self.send(1, x, ys, self.at((x + d) % 4, y), self.b2.at[4 - d])

    def column(self, o):
        arrived(self.buf.at[pl.ds(0, 3), :, self.cols[0]], self.a2.at[o])
        if o:
            arrived(self.buf.at[pl.ds(0, 4), :, self.cols[1]], self.b2.at[o])

    def finish(self):
        arrived(self.buf.at[pl.ds(0, 15)], self.out)


def kernel(
    x_hbm, g1_hbm, w1_hbm, w2_hbm, g2_hbm, map_hbm, tpl_hbm, mult_hbm, sharp_ref,
    lg, lse_out,
    xv, g1v, g2v, multv, tok, w1, w2, part, r1a, r1b, s1a, s1b, r2a, r2b, mapv, emb, tplv, shc, gs, zr, zs, cls,
    lse_mine, lse_in,
    load_sem, w_send, w_recv, g_a1, g_a2, g_b1, g_b2, g_out, e_a1, e_a2, e_b1, e_b2, e_out,
    ra1, rb1, ra2, rb2, rs_out, z_recv, z_out, za_recv, za_out, pair_recv, pair_out, l_recv, l_out,
):
    m = lax.axis_index("cls")
    z = lax.axis_index("img")
    x, y, c = m // 8, (m // 2) % 4, m % 2
    me = x * 4 + y
    width, edim = tok.shape[-1], emb.shape[-1]

    def at(xx, yy, cc=None):
        return (z, (xx * 4 + yy) * 2 + (c if cc is None else cc))

    mate = at(x, y, 1 - c)
    z_up, z_down = ((z + 1) % 8, m), ((z + 7) % 8, m)

    def send(src, dst, s_sem, r_sem, to):
        pltpu.make_async_remote_copy(
            src_ref=src, dst_ref=dst, send_sem=s_sem, recv_sem=r_sem, device_id=to, device_id_type=MESH
        ).start()

    barrier = pltpu.get_barrier_semaphore()
    x_peers = [at((x + d) % 4, y) for d in ORDER]
    x_others = [at((x + d) % 4, y, 1 - c) for d in ORDER]
    y_peers = [at(x, (y + d) % 4) for d in ORDER]
    partners = x_peers + y_peers + [mate, z_up, z_down] + x_others
    for to in partners:
        pl.semaphore_signal(barrier, inc=1, device_id=to, device_id_type=MESH)

    loads = [
        pltpu.make_async_copy(src, dst, load_sem.at[i])
        for i, (src, dst) in enumerate(
            (
                (x_hbm, xv), (g1_hbm, g1v), (mult_hbm, multv), (tpl_hbm, tplv),
                (w1_hbm, w1.at[c]), (w2_hbm, w2.at[c]), (g2_hbm, g2v), (map_hbm, mapv),
            )
        )
    ]
    for load in loads:
        load.start()

    loads[0].wait()
    loads[1].wait()
    states = xv[...].astype(F32)
    normed = layer_norm(states, g1v[...][None, :]).astype(BF16)
    tok[0, me] = normed[:16]
    tok[1, me] = normed[16:]

    loads[2].wait()
    weights = multv[...].astype(F32)
    total = jnp.sum(weights, axis=0, keepdims=True)
    row_id = lax.broadcasted_iota(jnp.int32, weights.shape, 0)
    for t in range(2):
        own = jnp.sum(jnp.where(row_id == 2 * z + t, weights, 0.0), axis=0, keepdims=True)
        portion = own / total
        for q in range(4):
            shc[t, pl.ds(q * 128, 128), :] = jnp.broadcast_to(portion[:, q * 128 : (q + 1) * 128], (128, 128)).T

    pl.semaphore_wait(barrier, len(partners))

    splits = (896, 768)
    gather = [
        PlaneGather(
            x, y, at, tok.at[h], splits[h], (g_a1.at[h], g_a2.at[h], g_b1.at[h], g_b2.at[h], g_out.at[h])
        )
        for h in range(2)
    ]
    gather[0].start()
    send(w1_hbm, w1.at[c], w_send.at[0], w_recv.at[0], mate)
    send(w2_hbm, w2.at[c], w_send.at[1], w_recv.at[1], mate)

    def group_sums(*offsets):
        for off in offsets:
            k = (z + off) % 8

            @pl.loop(0, 2)
            def _(i):
                rows = pl.ds(k * 64 + i * 32, 32)
                acc = None
                for t in range(2):
                    tmpl = tplv[rows, t, :].astype(F32)
                    coef = shc[t, rows, 0:1] * lax.rsqrt(jnp.sum(tmpl * tmpl, axis=-1, keepdims=True) + 1e-06)
                    acc = coef * tmpl if acc is None else acc + coef * tmpl
                gs[k, pl.ds(i * 32, 32), :] = acc.astype(BF16)

    halves = (pl.ds(0, 640), pl.ds(640, 640))

    def z_reduce(s):
        for way, half in ((0, 0), (1, 1), (0, 1), (1, 0)):
            if s == 0 and way != half:
                continue
            cols = halves[half]
            k = (z + 4 + s) % 8 if way == 0 else (z + 4 - s + 8) % 8
            first = s == 0 or (s == 1 and way != half)
            if first:
                src = gs.at[k, :, cols]
            else:
                came = zr.at[way, s - 1, :, cols]
                arrived(came, z_recv.at[way, half, s - 1])
                zs[way, s, :, cols] = (gs[k, :, cols].astype(F32) + came[...].astype(F32)).astype(BF16)
                src = zs.at[way, s, :, cols]
            send(src, zr.at[way, s, :, cols], z_out, z_recv.at[way, half, s], z_down if way == 0 else z_up)

    def z_total():
        for half in range(2):
            cols = halves[half]
            for way in range(2):
                arrived(zr.at[way, 3, :, cols], z_recv.at[way, half, 3])
            cls[z, :, cols] = (
                gs[z, :, cols].astype(F32) + zr[0, 3, :, cols].astype(F32) + zr[1, 3, :, cols].astype(F32)
            ).astype(BF16)

    def z_gather(s):
        for way, half in ((0, 0), (1, 1), (0, 1), (1, 0)):
            cols = halves[half]
            far = 4 if way == half else 3
            k = (z + s) % 8 if way == 0 else (z - s + 8) % 8
            if s > far:
                continue
            chunk = cls.at[k, :, cols]
            if s > 0:
                arrived(chunk, za_recv.at[way, half, s - 1])
            if s < far:
                send(chunk, chunk, za_out, za_recv.at[way, half, s], z_down if way == 0 else z_up)

    def ffn(h):
        for o in range(4):
            gather[h].column(o)
        rows = tok[h].reshape(256, width)
        hidden = []
        for k in range(2):
            pre = jnp.dot(rows, w1[k], preferred_element_type=F32)
            hidden.append((pre * 0.5 * (1.0 + lax.erf(pre * 0.7071067811865476))).astype(BF16))
        out = jnp.dot(hidden[0], w2[0], preferred_element_type=F32)
        out = out + jnp.dot(hidden[1], w2[1], preferred_element_type=F32)
        part[h] = out.astype(BF16).reshape(16, 16, width)
        cols = gather[h].cols
        first = pl.ds(0, splits[h])
        second = pl.ds(0, width - splits[h])
        for o in ORDER + (0,):
            xs = (x + o) % 4
            for d in ORDER:
                yd = (y + d) % 4
                send(
                    part.at[h, xs * 4 + yd, :, cols[0]], r1a.at[h, 3 - d, o, :, first],
                    rs_out.at[h, 0], ra1.at[h, o], at(x, yd),
                )
            if o:
                send(
                    part.at[h, pl.ds(xs * 4, 4), :, cols[1]], r1b.at[h, 3 - o, :, :, second],
                    rs_out.at[h, 1], rb1.at[h, 3 - o], at(xs, y),
                )

    def second_stage(h):
        cols = gather[h].cols
        first = pl.ds(0, splits[h])
        second = pl.ds(0, width - splits[h])
        for o in ORDER:
            xs = (x + o) % 4
            arrived(r1a.at[h, :, o, :, first], ra1.at[h, o])
            total = part[h, xs * 4 + y, :, cols[0]].astype(F32)
            for k in range(3):
                total = total + r1a[h, k, o, :, first].astype(F32)
            s1a[h, o, :, first] = total.astype(BF16)
            send(s1a.at[h, o, :, first], r2a.at[h, 3 - o, :, first], rs_out.at[h, 2], ra2.at[h], at(xs, y))
        for k in range(3):
            arrived(r1b.at[h, k, :, :, second], rb1.at[h, k])
        for o in ORDER:
            ys = (y + o) % 4
            total = part[h, x * 4 + ys, :, cols[1]].astype(F32)
            for k in range(3):
                total = total + r1b[h, k, ys, :, second].astype(F32)
            s1b[h, o, :, second] = total.astype(BF16)
            send(s1b.at[h, o, :, second], r2b.at[h, 3 - o, :, second], rs_out.at[h, 3], rb2.at[h], at(x, ys))

    def embed(h):
        cols = gather[h].cols
        first = pl.ds(0, splits[h])
        second = pl.ds(0, width - splits[h])
        own_a = part[h, me, :, cols[0]].astype(F32)
        own_b = part[h, me, :, cols[1]].astype(F32)
        arrived(r1a.at[h, :, 0, :, first], ra1.at[h, 0])
        for k in range(3):
            own_a = own_a + r1a[h, k, 0, :, first].astype(F32)
            own_b = own_b + r1b[h, k, y, :, second].astype(F32)
        arrived(r2a.at[h, :, :, first], ra2.at[h])
        arrived(r2b.at[h, :, :, second], rb2.at[h])
        for k in range(3):
            own_a = own_a + r2a[h, k, :, first].astype(F32)
            own_b = own_b + r2b[h, k, :, second].astype(F32)
        stream = xv[pl.ds(h * 16, 16), :].astype(F32) + jnp.concatenate([own_a, own_b], axis=1)
        pooled = layer_norm(stream, g2v[...][None, :]).astype(BF16)
        projected = jnp.dot(pooled, mapv[...], preferred_element_type=F32)
        emb[c, h, me] = (
            projected * lax.rsqrt(jnp.sum(projected * projected, axis=-1, keepdims=True) + 1e-06)
        ).astype(BF16)
        spread[h].start()

    spread = [
        PlaneGather(
            x, y, at, emb.at[c, h], edim // 2, (e_a1.at[h], e_a2.at[h], e_b1.at[h], e_b2.at[h], e_out.at[h])
        )
        for h in range(2)
    ]

    def to_mate(h):
        for o in (0, 1, 3, 2):
            spread[h].column(o)
            quad = emb.at[c, h, pl.ds(((x + o) % 4) * 4, 4)]
            send(quad, quad, pair_out.at[h], pair_recv.at[h], mate)

    sharp = sharp_ref[0]

    def logits(core, h):
        rows = emb[core, h].reshape(256, edim)
        classes = cls[...].reshape(512, edim)
        val = sharp * lax.dot_general(rows, classes, (((1,), (1,)), ((), ())), preferred_element_type=F32)
        lg[:, core, h] = val.reshape(16, 16, 512)
        top = jnp.max(val, axis=-1, keepdims=True)
        lse = top + jnp.log(jnp.sum(jnp.exp(val - top), axis=-1, keepdims=True))
        for q in range(2):
            half = jnp.broadcast_to(lse[q * 128 : (q + 1) * 128], (128, 128)).T
            lse_mine[0, pl.ds((h * 2 + core) * 2 + q, 1), :] = half[0:1, :]

    loads[3].wait()
    group_sums(4)
    z_reduce(0)
    gather[0].forward()
    gather[1].start()
    group_sums(5, 3)
    z_reduce(1)
    group_sums(6, 2)
    gather[1].forward()
    group_sums(7, 1, 0)
    z_reduce(2)
    for i in (4, 5, 6, 7):
        loads[i].wait()
    arrived(w1.at[1 - c], w_recv.at[0])
    arrived(w2.at[1 - c], w_recv.at[1])
    ffn(0)
    z_reduce(3)
    ffn(1)
    second_stage(0)
    z_total()
    z_gather(0)
    second_stage(1)
    embed(0)
    z_gather(1)
    spread[0].forward()
    embed(1)
    z_gather(2)
    spread[1].forward()
    to_mate(0)
    z_gather(3)
    z_gather(4)
    logits(c, 0)
    arrived(emb.at[1 - c, 0], pair_recv.at[0])
    logits(1 - c, 0)
    to_mate(1)
    logits(c, 1)
    arrived(emb.at[1 - c, 1], pair_recv.at[1])
    logits(1 - c, 1)

    def merge(values):
        top = values[0]
        for v in values[1:]:
            top = jnp.maximum(top, v)
        acc = jnp.exp(values[0] - top)
        for v in values[1:]:
            acc = acc + jnp.exp(v - top)
        return top + jnp.log(acc)

    for i, d in enumerate(ORDER):
        send(lse_mine.at[0], lse_in.at[4 - d], l_out.at[0], l_recv.at[4 - d], x_peers[i])
        send(lse_mine.at[0], lse_in.at[8 - d], l_out.at[0], l_recv.at[8 - d], x_others[i])
    send(lse_mine.at[0], lse_in.at[0], l_out.at[0], l_recv.at[0], mate)
    for i in range(8):
        if i != 4:
            arrived(lse_in.at[i], l_recv.at[i])
    lse_mine[1] = merge([lse_mine[0]] + [lse_in[i] for i in range(8) if i != 4])
    for i, d in enumerate(ORDER):
        send(lse_mine.at[1], lse_in.at[8 + 4 - d], l_out.at[1], l_recv.at[8 + 4 - d], y_peers[i])

    for h in range(2):
        cols = gather[h].cols
        gather[h].finish()
        spread[h].finish()
        arrived(part.at[h, pl.ds(0, 12), :, cols[0]], rs_out.at[h, 0])
        arrived(part.at[h, pl.ds(0, 12), :, cols[1]], rs_out.at[h, 1])
        arrived(part.at[h, pl.ds(0, 3), :, cols[0]], rs_out.at[h, 2])
        arrived(part.at[h, pl.ds(0, 3), :, cols[1]], rs_out.at[h, 3])
        arrived(emb.at[c, h], pair_out.at[h])
    arrived(w1.at[c], w_send.at[0])
    arrived(w2.at[c], w_send.at[1])
    arrived(gs.at[pl.ds(0, 7)], z_out)
    arrived(gs.at[pl.ds(0, 7)], za_out)
    arrived(lse_in.at[pl.ds(0, 7)], l_out.at[0])

    for d in ORDER:
        arrived(lse_in.at[8 + d], l_recv.at[8 + d])
    lse = merge([lse_mine[1]] + [lse_in[8 + d] for d in ORDER])
    for h in range(2):
        for core in range(2):
            for q in range(2):
                row = (h * 2 + core) * 2 + q
                columns = jnp.broadcast_to(lse[row : row + 1, :], (128, 128)).T
                lse_out[pl.ds(q * 8, 8), core, h] = columns.reshape(8, 16, 128)
    arrived(lse_in.at[pl.ds(0, 3)], l_out.at[1])


def shards(states, gain1, w1, w2, gain2, mapper, prompts, multiplicity, sharpness):
    width = states.shape[1]
    edim = mapper.shape[1]
    hbm = pl.BlockSpec(memory_space=pltpu.HBM)
    vmem = pl.BlockSpec(memory_space=pltpu.VMEM)
    dma = pltpu.SemaphoreType.DMA
    logit, lse = pl.pallas_call(
        kernel,
        name="whole",
        out_shape=(pltpu.VMEM((16, 2, 2, 16, 512), F32), pltpu.VMEM((16, 2, 2, 16, 128), F32)),
        in_specs=[hbm] * 8 + [pl.BlockSpec(memory_space=pltpu.SMEM)],
        out_specs=(vmem, vmem),
        scratch_shapes=[
            pltpu.VMEM((32, width), BF16),
            pltpu.VMEM((width,), F32),
            pltpu.VMEM((width,), F32),
            pltpu.VMEM((16, 512), jnp.int32),
            pltpu.VMEM((2, 16, 16, width), BF16),
            pltpu.VMEM((2, width, 256), BF16),
            pltpu.VMEM((2, 256, width), BF16),
            pltpu.VMEM((2, 16, 16, width), BF16),
            pltpu.VMEM((2, 3, 4, 16, 896), BF16),
            pltpu.VMEM((2, 3, 4, 16, 896), BF16),
            pltpu.VMEM((2, 4, 16, 896), BF16),
            pltpu.VMEM((2, 4, 16, 896), BF16),
            pltpu.VMEM((2, 3, 16, 896), BF16),
            pltpu.VMEM((2, 3, 16, 896), BF16),
            pltpu.VMEM((width, edim), BF16),
            pltpu.VMEM((2, 2, 16, 16, edim), BF16),
            pltpu.VMEM((512, 2, edim), BF16),
            pltpu.VMEM((2, 512, 128), F32),
            pltpu.VMEM((8, 64, edim), BF16),
            pltpu.VMEM((2, 4, 64, edim), BF16),
            pltpu.VMEM((2, 4, 64, edim), BF16),
            pltpu.VMEM((8, 64, edim), BF16),
            pltpu.VMEM((2, 8, 128), F32),
            pltpu.VMEM((12, 8, 128), F32),
            dma((8,)), dma((2,)), dma((2,)),
            dma((2, 4)), dma((2, 4)), dma((2, 4)), dma((2, 4)), dma((2,)),
            dma((2, 4)), dma((2, 4)), dma((2, 4)), dma((2, 4)), dma((2,)),
            dma((2, 4)), dma((2, 3)), dma((2,)), dma((2,)), dma((2, 4)),
            dma((2, 2, 4)), dma(()), dma((2, 2, 4)), dma(()),
            dma((2,)), dma((2,)),
            dma((12,)), dma((2,)),
        ],
        compiler_params=pltpu.CompilerParams(
            collective_id=0, has_side_effects=True, vmem_limit_bytes=61 * 1024 * 1024
        ),
    )(states, gain1, w1, w2, gain2, mapper, prompts, multiplicity.T, sharpness)
    return logit.reshape(1024, 512) - lse.reshape(1024, 128)[:, :1]


def solution(mesh):
    in_specs = (
        P(("img", "cls"), None),
        P(),
        P(None, "cls"),
        P("cls", None),
        P(),
        P(),
        P("cls", "img", None),
        P("cls", None),
        P(),
    )
    out_specs = P("img", "cls")
    return jax.shard_map(shards, mesh=mesh, in_specs=in_specs, out_specs=out_specs, check_vma=False)
```

```python
import jax
import jax.numpy as jnp
from jax import lax
from jax.experimental import pallas as pl
from jax.experimental.pallas import tpu as pltpu
from jax.sharding import PartitionSpec as P

MESH = pl.DeviceIdType.MESH
F32 = jnp.float32
BF16 = jnp.bfloat16
ORDER = (1, 3, 2)


def layer_norm(values, gain):
    center = values - jnp.mean(values, axis=-1, keepdims=True)
    variance = jnp.mean(center * center, axis=-1, keepdims=True)
    return center * lax.rsqrt(variance + 1e-05) * gain


def arrived(ref, sem):
    pltpu.make_async_copy(ref, ref, sem).wait()


class PlaneGather:
    def __init__(self, u, v, at, buf, sems, relayed):
        self.u, self.v, self.at, self.buf, self.relayed = u, v, at, buf, relayed
        self.first, self.second, self.third, self.out = sems

    def send(self, uu, vv, to, sem):
        piece = self.buf.at[uu * 4 + vv]
        pltpu.make_async_remote_copy(
            src_ref=piece, dst_ref=piece, send_sem=self.out, recv_sem=sem, device_id=to, device_id_type=MESH
        ).start()

    def start(self):
        for d in ORDER:
            self.send(self.u, self.v, self.at((self.u + d) % 4, self.v), self.first.at[4 - d])

    def forward(self, o):
        u, v = self.u, self.v
        uo = (u + o) % 4
        if o:
            arrived(self.buf.at[uo * 4 + v], self.first.at[o])
        self.send(uo, v, self.at(u, (v + 1) % 4), self.second.at[o, 0])
        self.send(uo, v, self.at(u, (v + 3) % 4), self.second.at[o, 1])
        if o not in self.relayed:
            self.send(uo, v, self.at(u, (v + 2) % 4), self.third.at[o])

    def relay(self, o):
        u, v = self.u, self.v
        came, to = (3, 1) if o % 2 == 0 else (1, 3)
        uo, vs = (u + o) % 4, (v + came) % 4
        arrived(self.buf.at[uo * 4 + vs], self.second.at[o, o % 2])
        self.send(uo, vs, self.at(u, (v + to) % 4), self.third.at[o])

    def column(self, o):
        uo = (self.u + o) % 4
        for side, d in ((0, 3), (1, 1)):
            if o not in self.relayed or side != o % 2:
                arrived(self.buf.at[uo * 4 + (self.v + d) % 4], self.second.at[o, side])
        arrived(self.buf.at[uo * 4 + (self.v + 2) % 4], self.third.at[o])

    def finish(self):
        arrived(self.buf.at[pl.ds(0, 15)], self.out)


def kernel(
    x_hbm, g1_hbm, w1_hbm, w2_hbm, g2_hbm, map_hbm, tpl_hbm, mult_hbm, sharp_ref,
    lg, lse_out,
    xv, g1v, g2v, multv, tok, w1, w2, part, r1, s1, r2, mapv, emb, tplv, shc, gs, zr, zs, cls,
    stage, lse_x, lse_y,
    load_sem, w_send, w_recv, g_1, g_2, g_3, g_out, e_1, e_2, e_3, e_out,
    r1_recv, r2_recv, rs_out, z_recv, z_out, za_recv, za_out, pair_recv, pair_out, lg_recv, lg_out, lx_recv, ly_recv, l_out,
):
    m = lax.axis_index("cls")
    z = lax.axis_index("img")
    x, y, c = m // 8, (m // 2) % 4, m % 2
    u, v = x + c * (y - x), y + c * (x - y)
    me = u * 4 + v
    width, edim = tok.shape[-1], emb.shape[-1]

    def device(xx, yy, cc):
        return (z, (xx * 4 + yy) * 2 + cc)

    def at(uu, vv):
        return device(uu + c * (vv - uu), vv + c * (uu - vv), c)

    mate = device(x, y, 1 - c)
    z_up, z_down = ((z + 1) % 8, m), ((z + 7) % 8, m)

    def send(src, dst, s_sem, r_sem, to):
        pltpu.make_async_remote_copy(
            src_ref=src, dst_ref=dst, send_sem=s_sem, recv_sem=r_sem, device_id=to, device_id_type=MESH
        ).start()

    barrier = pltpu.get_barrier_semaphore()
    x_peers = [device((x + d) % 4, y, c) for d in ORDER]
    y_peers = [device(x, (y + d) % 4, c) for d in ORDER]
    y_others = [device(x, (y + d) % 4, 1 - c) for d in ORDER]
    partners = x_peers + y_peers + [mate, z_up, z_down] + y_others
    for to in partners:
        pl.semaphore_signal(barrier, inc=1, device_id=to, device_id_type=MESH)

    loads = [
        pltpu.make_async_copy(src, dst, load_sem.at[i])
        for i, (src, dst) in enumerate(
            (
                (x_hbm, xv), (g1_hbm, g1v), (mult_hbm, multv), (tpl_hbm, tplv),
                (w1_hbm, w1.at[c]), (w2_hbm, w2.at[c]), (g2_hbm, g2v), (map_hbm, mapv),
            )
        )
    ]
    for load in loads:
        load.start()

    loads[0].wait()
    loads[1].wait()
    states = xv[...].astype(F32)
    normed = layer_norm(states, g1v[...][None, :]).astype(BF16)
    tok[0, me] = normed[:16]
    tok[1, me] = normed[16:]

    loads[2].wait()
    weights = multv[...].astype(F32)
    total = jnp.sum(weights, axis=0, keepdims=True)
    row_id = lax.broadcasted_iota(jnp.int32, weights.shape, 0)
    for t in range(2):
        own = jnp.sum(jnp.where(row_id == 2 * z + t, weights, 0.0), axis=0, keepdims=True)
        portion = own / total
        for q in range(4):
            shc[t, pl.ds(q * 128, 128), :] = jnp.broadcast_to(portion[:, q * 128 : (q + 1) * 128], (128, 128)).T

    def group_sums(*offsets):
        for off in offsets:
            k = (z + off) % 8

            @pl.loop(0, 2)
            def _(i):
                rows = pl.ds(k * 64 + i * 32, 32)
                acc = None
                for t in range(2):
                    tmpl = tplv[rows, t, :].astype(F32)
                    coef = shc[t, rows, 0:1] * lax.rsqrt(jnp.sum(tmpl * tmpl, axis=-1, keepdims=True) + 1e-06)
                    acc = coef * tmpl if acc is None else acc + coef * tmpl
                gs[k, pl.ds(i * 32, 32), :] = acc.astype(BF16)

    loads[3].wait()
    group_sums(4)
    pl.semaphore_wait(barrier, len(partners))

    gather = [PlaneGather(u, v, at, tok.at[h], (g_1.at[h], g_2.at[h], g_3.at[h], g_out.at[h]), ()) for h in range(2)]
    halves = (pl.ds(0, 640), pl.ds(640, 640))

    def z_reduce(s):
        for way, half in ((0, 0), (1, 1), (0, 1), (1, 0)):
            if s == 0 and way != half:
                continue
            cols = halves[half]
            k = (z + 4 + s) % 8 if way == 0 else (z + 4 - s + 8) % 8
            first = s == 0 or (s == 1 and way != half)
            if first:
                src = gs.at[k, :, cols]
            else:
                came = zr.at[way, s - 1, :, cols]
                arrived(came, z_recv.at[way, half, s - 1])
                zs[way, s, :, cols] = (gs[k, :, cols].astype(F32) + came[...].astype(F32)).astype(BF16)
                src = zs.at[way, s, :, cols]
            send(src, zr.at[way, s, :, cols], z_out, z_recv.at[way, half, s], z_down if way == 0 else z_up)

    def to_mate(k):
        send(cls.at[c, k], cls.at[c, k], pair_out, pair_recv, mate)

    def z_total():
        for half in range(2):
            cols = halves[half]
            for way in range(2):
                arrived(zr.at[way, 3, :, cols], z_recv.at[way, half, 3])
            cls[c, z, :, cols] = (
                gs[z, :, cols].astype(F32) + zr[0, 3, :, cols].astype(F32) + zr[1, 3, :, cols].astype(F32)
            ).astype(BF16)

    def z_gather(s):
        for way, half in ((0, 0), (1, 1), (0, 1), (1, 0)):
            cols = halves[half]
            far = 4 if way == half else 3
            k = (z + s) % 8 if way == 0 else (z - s + 8) % 8
            if s > far:
                continue
            chunk = cls.at[c, k, :, cols]
            if s > 0:
                arrived(chunk, za_recv.at[way, half, s - 1])
            if s < far:
                send(chunk, chunk, za_out, za_recv.at[way, half, s], z_down if way == 0 else z_up)
        for k in {0: (0,), 4: (4,)}.get(s, (s, 8 - s)):
            to_mate((z + k) % 8)

    def ffn(h):
        for o in range(4):
            gather[h].column(o)
        rows = tok[h].reshape(256, width)
        hidden = []
        for k in range(2):
            pre = jnp.dot(rows, w1[k], preferred_element_type=F32)
            hidden.append((pre * 0.5 * (1.0 + lax.erf(pre * 0.7071067811865476))).astype(BF16))
        out = jnp.dot(hidden[0], w2[0], preferred_element_type=F32)
        out = out + jnp.dot(hidden[1], w2[1], preferred_element_type=F32)
        part[h] = out.astype(BF16).reshape(16, 16, width)

    def first_stage(h):
        for o in ORDER + (0,):
            for d in ORDER:
                vd = (v + d) % 4
                send(
                    part.at[h, ((u + o) % 4) * 4 + vd], r1.at[h, 3 - d, o],
                    rs_out.at[h, 0], r1_recv.at[h, o], at(u, vd),
                )

    def second_stage(h, o):
        uo = (u + o) % 4
        arrived(r1.at[h, :, o], r1_recv.at[h, o])
        total = part[h, uo * 4 + v].astype(F32)
        for k in range(3):
            total = total + r1[h, k, o].astype(F32)
        s1[h, o] = total.astype(BF16)
        send(s1.at[h, o], r2.at[h, 3 - o], rs_out.at[h, 1], r2_recv.at[h], at(uo, v))

    def embed(h):
        total = part[h, me].astype(F32)
        arrived(r1.at[h, :, 0], r1_recv.at[h, 0])
        for k in range(3):
            total = total + r1[h, k, 0].astype(F32)
        arrived(r2.at[h], r2_recv.at[h])
        for k in range(3):
            total = total + r2[h, k].astype(F32)
        stream = xv[pl.ds(h * 16, 16), :].astype(F32) + total
        pooled = layer_norm(stream, g2v[...][None, :]).astype(BF16)
        projected = jnp.dot(pooled, mapv[...], preferred_element_type=F32)
        emb[h, me] = (
            projected * lax.rsqrt(jnp.sum(projected * projected, axis=-1, keepdims=True) + 1e-06)
        ).astype(BF16)

    spread = [PlaneGather(u, v, at, emb.at[h], (e_1.at[h], e_2.at[h], e_3.at[h], e_out.at[h]), ()) for h in range(2)]

    sharp = sharp_ref[0]

    def logits(h):
        for o in range(4):
            spread[h].column(o)
        rows = emb[h].reshape(256, edim)
        vals = []
        for core in (1 - c, c):
            classes = cls[core].reshape(512, edim)
            val = sharp * lax.dot_general(rows, classes, (((1,), (1,)), ((), ())), preferred_element_type=F32)
            for j in range(16):
                uu, vv = j // 4, j % 4
                place = (uu + c * (vv - uu)) * 4 + vv + c * (uu - vv)
                piece = val[j * 16 : (j + 1) * 16]
                if vals:
                    lg[place, c, h] = piece
                else:
                    stage[h, j] = piece
                    send(stage.at[h, j], lg.at[place, c, h], lg_out, lg_recv, mate)
            vals.append(val)
        top = jnp.maximum(jnp.max(vals[0], axis=-1, keepdims=True), jnp.max(vals[1], axis=-1, keepdims=True))
        total = jnp.sum(jnp.exp(vals[0] - top) + jnp.exp(vals[1] - top), axis=-1, keepdims=True)
        lse = top + jnp.log(total)
        for q in range(2):
            half = jnp.broadcast_to(lse[q * 128 : (q + 1) * 128], (128, 128)).T
            lse_x[0, h * 2 + q : h * 2 + q + 1, :] = half[0:1, :]

    z_reduce(0)
    gather[0].start()
    send(w1_hbm, w1.at[c], w_send.at[0], w_recv.at[0], mate)
    send(w2_hbm, w2.at[c], w_send.at[1], w_recv.at[1], mate)
    group_sums(2)
    gather[0].forward(0)
    group_sums(5)
    group_sums(7)
    gather[1].start()
    gather[0].forward(1)
    group_sums(3)
    z_reduce(1)
    gather[0].forward(2)
    gather[0].forward(3)
    group_sums(1)
    group_sums(6)
    gather[1].forward(0)
    gather[1].forward(3)
    gather[1].forward(2)
    gather[1].forward(1)
    group_sums(0)
    z_reduce(2)
    for i in (4, 5, 6, 7):
        loads[i].wait()
    arrived(w1.at[1 - c], w_recv.at[0])
    arrived(w2.at[1 - c], w_recv.at[1])
    ffn(0)
    first_stage(0)
    z_reduce(3)
    ffn(1)
    first_stage(1)
    z_total()
    z_gather(0)
    second_stage(0, 2)
    second_stage(0, 3)
    second_stage(0, 1)
    z_gather(1)
    second_stage(1, 2)
    second_stage(1, 1)
    second_stage(1, 3)
    embed(0)
    spread[0].start()
    spread[0].forward(0)
    z_gather(2)
    embed(1)
    spread[1].start()
    spread[1].forward(0)
    spread[0].forward(2)
    spread[0].forward(1)
    z_gather(3)
    spread[0].forward(3)
    spread[1].forward(2)
    spread[1].forward(3)
    z_gather(4)
    spread[1].forward(1)
    arrived(cls.at[1 - c], pair_recv)
    logits(0)
    logits(1)

    def merge(values):
        top = values[0]
        for v in values[1:]:
            top = jnp.maximum(top, v)
        acc = jnp.exp(values[0] - top)
        for v in values[1:]:
            acc = acc + jnp.exp(v - top)
        return top + jnp.log(acc)

    for i, d in enumerate(ORDER):
        send(lse_x.at[0], lse_x.at[4 - d], l_out.at[0], lx_recv.at[4 - d], x_peers[i])
    for d in ORDER:
        arrived(lse_x.at[d], lx_recv.at[d])
    lse_y[c, 0] = merge([lse_x[i] for i in range(4)])
    mine = lse_y.at[c, 0]
    for i, d in enumerate(ORDER):
        send(mine, lse_y.at[c, 4 - d], l_out.at[1], ly_recv.at[c, 4 - d], y_peers[i])
        send(mine, lse_y.at[c, 4 - d], l_out.at[1], ly_recv.at[c, 4 - d], y_others[i])
    send(mine, mine, l_out.at[1], ly_recv.at[c, 0], mate)

    for h in range(2):
        gather[h].finish()
        spread[h].finish()
        arrived(part.at[h, pl.ds(0, 12)], rs_out.at[h, 0])
        arrived(r2.at[h], rs_out.at[h, 1])
    arrived(w1.at[c], w_send.at[0])
    arrived(w2.at[c], w_send.at[1])
    arrived(gs.at[pl.ds(0, 7)], z_out)
    arrived(gs.at[pl.ds(0, 7)], za_out)
    arrived(cls.at[c], pair_out)
    arrived(stage, lg_out)
    arrived(lse_x.at[pl.ds(0, 3)], l_out.at[0])
    arrived(lg.at[:, 1 - c], lg_recv)

    arrived(lse_y.at[1 - c, 0], ly_recv.at[1 - c, 0])
    for d in ORDER:
        for core in (c, 1 - c):
            arrived(lse_y.at[core, d], ly_recv.at[core, d])
    for core in range(2):
        lse = merge([lse_y[core, i] for i in range(4)])
        for row in range(4):
            columns = jnp.broadcast_to(lse[row : row + 1, :], (128, 128)).T
            for k in range(8):
                j = (row % 2) * 8 + k
                place = (j % 4) * 4 + j // 4 if core else j
                lse_out[place, core, row // 2] = columns[k * 16 : (k + 1) * 16]
    arrived(lse_y.at[0, pl.ds(0, 3)], l_out.at[1])
    arrived(lse_y.at[0], l_out.at[1])


def shards(states, gain1, w1, w2, gain2, mapper, prompts, multiplicity, sharpness):
    width = states.shape[1]
    edim = mapper.shape[1]
    hbm = pl.BlockSpec(memory_space=pltpu.HBM)
    vmem = pl.BlockSpec(memory_space=pltpu.VMEM)
    dma = pltpu.SemaphoreType.DMA
    logit, lse = pl.pallas_call(
        kernel,
        name="whole",
        out_shape=(pltpu.VMEM((16, 2, 2, 16, 512), F32), pltpu.VMEM((16, 2, 2, 16, 128), F32)),
        in_specs=[hbm] * 8 + [pl.BlockSpec(memory_space=pltpu.SMEM)],
        out_specs=(vmem, vmem),
        scratch_shapes=[
            pltpu.VMEM((32, width), BF16),
            pltpu.VMEM((width,), F32),
            pltpu.VMEM((width,), F32),
            pltpu.VMEM((16, 512), jnp.int32),
            pltpu.VMEM((2, 16, 16, width), BF16),
            pltpu.VMEM((2, width, 256), BF16),
            pltpu.VMEM((2, 256, width), BF16),
            pltpu.VMEM((2, 16, 16, width), BF16),
            pltpu.VMEM((2, 3, 4, 16, width), BF16),
            pltpu.VMEM((2, 4, 16, width), BF16),
            pltpu.VMEM((2, 3, 16, width), BF16),
            pltpu.VMEM((width, edim), BF16),
            pltpu.VMEM((2, 16, 16, edim), BF16),
            pltpu.VMEM((512, 2, edim), BF16),
            pltpu.VMEM((2, 512, 128), F32),
            pltpu.VMEM((8, 64, edim), BF16),
            pltpu.VMEM((2, 4, 64, edim), BF16),
            pltpu.VMEM((2, 4, 64, edim), BF16),
            pltpu.VMEM((2, 8, 64, edim), BF16),
            pltpu.VMEM((2, 16, 16, 512), F32),
            pltpu.VMEM((4, 4, 128), F32),
            pltpu.VMEM((2, 4, 4, 128), F32),
            dma((8,)), dma((2,)), dma((2,)),
            dma((2, 4)), dma((2, 4, 2)), dma((2, 4)), dma((2,)),
            dma((2, 4)), dma((2, 4, 2)), dma((2, 4)), dma((2,)),
            dma((2, 4)), dma((2,)), dma((2, 2)),
            dma((2, 2, 4)), dma(()), dma((2, 2, 4)), dma(()),
            dma(()), dma(()), dma(()), dma(()),
            dma((4,)), dma((2, 4)), dma((2,)),
        ],
        compiler_params=pltpu.CompilerParams(
            collective_id=0, has_side_effects=True, vmem_limit_bytes=61 * 1024 * 1024
        ),
    )(states, gain1, w1, w2, gain2, mapper, prompts, multiplicity.T, sharpness)
    return logit.reshape(1024, 512) - lse.reshape(1024, 128)[:, :1]


def solution(mesh):
    in_specs = (
        P(("img", "cls"), None),
        P(),
        P(None, "cls"),
        P("cls", None),
        P(),
        P(),
        P("cls", "img", None),
        P("cls", None),
        P(),
    )
    out_specs = P("img", "cls")
    return jax.shard_map(shards, mesh=mesh, in_specs=in_specs, out_specs=out_specs, check_vma=False)
```

```python
import jax
import jax.numpy as jnp
from jax import lax
from jax.experimental import pallas as pl
from jax.experimental.pallas import tpu as pltpu
from jax.sharding import PartitionSpec as P

MESH = pl.DeviceIdType.MESH
F32 = jnp.float32
BF16 = jnp.bfloat16
ORDER = (1, 3, 2)


def layer_norm(values, gain):
    center = values - jnp.mean(values, axis=-1, keepdims=True)
    variance = jnp.mean(center * center, axis=-1, keepdims=True)
    return center * lax.rsqrt(variance + 1e-05) * gain


def arrived(ref, sem):
    pltpu.make_async_copy(ref, ref, sem).wait()


class PlaneGather:
    def __init__(self, u, v, at, buf, sems, relayed):
        self.u, self.v, self.at, self.buf, self.relayed = u, v, at, buf, relayed
        self.first, self.second, self.third, self.out = sems

    def send(self, uu, vv, to, sem):
        piece = self.buf.at[uu * 4 + vv]
        pltpu.make_async_remote_copy(
            src_ref=piece, dst_ref=piece, send_sem=self.out, recv_sem=sem, device_id=to, device_id_type=MESH
        ).start()

    def start(self):
        for d in ORDER:
            self.send(self.u, self.v, self.at((self.u + d) % 4, self.v), self.first.at[4 - d])

    def forward(self, o):
        u, v = self.u, self.v
        uo = (u + o) % 4
        if o:
            arrived(self.buf.at[uo * 4 + v], self.first.at[o])
        self.send(uo, v, self.at(u, (v + 1) % 4), self.second.at[o, 0])
        self.send(uo, v, self.at(u, (v + 3) % 4), self.second.at[o, 1])
        if o not in self.relayed:
            self.send(uo, v, self.at(u, (v + 2) % 4), self.third.at[o])

    def relay(self, o):
        u, v = self.u, self.v
        came, to = (3, 1) if o % 2 == 0 else (1, 3)
        uo, vs = (u + o) % 4, (v + came) % 4
        arrived(self.buf.at[uo * 4 + vs], self.second.at[o, o % 2])
        self.send(uo, vs, self.at(u, (v + to) % 4), self.third.at[o])

    def column(self, o):
        uo = (self.u + o) % 4
        for side, d in ((0, 3), (1, 1)):
            if o not in self.relayed or side != o % 2:
                arrived(self.buf.at[uo * 4 + (self.v + d) % 4], self.second.at[o, side])
        arrived(self.buf.at[uo * 4 + (self.v + 2) % 4], self.third.at[o])

    def finish(self):
        arrived(self.buf.at[pl.ds(0, 15)], self.out)


def kernel(
    x_hbm, g1_hbm, w1_hbm, w2_hbm, g2_hbm, map_hbm, tpl_hbm, mult_hbm, sharp_ref,
    lg, lse_out,
    xv, g1v, g2v, multv, tok, w1, w2, part, r1, s1, r2, mapv, emb, tplv, shc, gs, zr, zs, cls,
    stage, lse_x, lse_y,
    load_sem, w_send, w_recv, g_1, g_2, g_3, g_out, e_1, e_2, e_3, e_out,
    r1_recv, r2_recv, rs_out, z_recv, z_out, za_recv, za_out, pair_recv, pair_out, lg_recv, lg_out, lx_recv, ly_recv, l_out,
):
    m = lax.axis_index("cls")
    z = lax.axis_index("img")
    x, y, c = m // 8, (m // 2) % 4, m % 2
    u, v = x + c * (y - x), y + c * (x - y)
    me = u * 4 + v
    width, edim = tok.shape[-1], emb.shape[-1]

    def device(xx, yy, cc):
        return (z, (xx * 4 + yy) * 2 + cc)

    def at(uu, vv):
        return device(uu + c * (vv - uu), vv + c * (uu - vv), c)

    mate = device(x, y, 1 - c)
    z_up, z_down = ((z + 1) % 8, m), ((z + 7) % 8, m)

    def send(src, dst, s_sem, r_sem, to):
        pltpu.make_async_remote_copy(
            src_ref=src, dst_ref=dst, send_sem=s_sem, recv_sem=r_sem, device_id=to, device_id_type=MESH
        ).start()

    barrier = pltpu.get_barrier_semaphore()
    x_peers = [device((x + d) % 4, y, c) for d in ORDER]
    y_peers = [device(x, (y + d) % 4, c) for d in ORDER]
    y_others = [device(x, (y + d) % 4, 1 - c) for d in ORDER]
    partners = x_peers + y_peers + [mate, z_up, z_down] + y_others
    loads = [
        pltpu.make_async_copy(src, dst, load_sem.at[i])
        for i, (src, dst) in enumerate(
            (
                (x_hbm, xv), (g1_hbm, g1v), (mult_hbm, multv), (tpl_hbm, tplv),
                (w1_hbm, w1.at[c]), (w2_hbm, w2.at[c]), (g2_hbm, g2v), (map_hbm, mapv),
            )
        )
    ]
    loads[0].start()
    loads[1].start()
    for to in partners:
        pl.semaphore_signal(barrier, inc=1, device_id=to, device_id_type=MESH)
    for load in loads[2:]:
        load.start()

    loads[0].wait()
    loads[1].wait()
    states = xv[...].astype(F32)
    normed = layer_norm(states, g1v[...][None, :]).astype(BF16)
    tok[0, me] = normed[:16]
    tok[1, me] = normed[16:]

    def group_sums(*offsets):
        for off in offsets:
            k = (z + off) % 8

            @pl.loop(0, 2)
            def _(i):
                rows = pl.ds(k * 64 + i * 32, 32)
                acc = None
                for t in range(2):
                    tmpl = tplv[rows, t, :].astype(F32)
                    coef = shc[t, rows, 0:1] * lax.rsqrt(jnp.sum(tmpl * tmpl, axis=-1, keepdims=True) + 1e-06)
                    acc = coef * tmpl if acc is None else acc + coef * tmpl
                gs[k, pl.ds(i * 32, 32), :] = acc.astype(BF16)

    pl.semaphore_wait(barrier, len(partners))

    gather = [PlaneGather(u, v, at, tok.at[h], (g_1.at[h], g_2.at[h], g_3.at[h], g_out.at[h]), ()) for h in range(2)]
    def first_sums():
        loads[2].wait()
        weights = multv[...].astype(F32)
        total = jnp.sum(weights, axis=0, keepdims=True)
        row_id = lax.broadcasted_iota(jnp.int32, weights.shape, 0)
        for t in range(2):
            own = jnp.sum(jnp.where(row_id == 2 * z + t, weights, 0.0), axis=0, keepdims=True)
            portion = own / total
            for q in range(4):
                shc[t, pl.ds(q * 128, 128), :] = jnp.broadcast_to(portion[:, q * 128 : (q + 1) * 128], (128, 128)).T
        loads[3].wait()
        group_sums(4)

    halves = (pl.ds(0, 640), pl.ds(640, 640))

    def z_reduce(s):
        for way, half in ((0, 0), (1, 1), (0, 1), (1, 0)):
            if s == 0 and way != half:
                continue
            cols = halves[half]
            k = (z + 4 + s) % 8 if way == 0 else (z + 4 - s + 8) % 8
            first = s == 0 or (s == 1 and way != half)
            if first:
                src = gs.at[k, :, cols]
            else:
                came = zr.at[way, s - 1, :, cols]
                arrived(came, z_recv.at[way, half, s - 1])
                zs[way, s, :, cols] = (gs[k, :, cols].astype(F32) + came[...].astype(F32)).astype(BF16)
                src = zs.at[way, s, :, cols]
            send(src, zr.at[way, s, :, cols], z_out, z_recv.at[way, half, s], z_down if way == 0 else z_up)

    def to_mate(k):
        send(cls.at[c, k], cls.at[c, k], pair_out, pair_recv, mate)

    def z_total():
        for half in range(2):
            cols = halves[half]
            for way in range(2):
                arrived(zr.at[way, 3, :, cols], z_recv.at[way, half, 3])
            cls[c, z, :, cols] = (
                gs[z, :, cols].astype(F32) + zr[0, 3, :, cols].astype(F32) + zr[1, 3, :, cols].astype(F32)
            ).astype(BF16)

    def z_gather(s):
        for way, half in ((0, 0), (1, 1), (0, 1), (1, 0)):
            cols = halves[half]
            far = 4 if way == half else 3
            k = (z + s) % 8 if way == 0 else (z - s + 8) % 8
            if s > far:
                continue
            chunk = cls.at[c, k, :, cols]
            if s > 0:
                arrived(chunk, za_recv.at[way, half, s - 1])
            if s < far:
                send(chunk, chunk, za_out, za_recv.at[way, half, s], z_down if way == 0 else z_up)
        for k in {0: (0,), 4: (4,)}.get(s, (s, 8 - s)):
            to_mate((z + k) % 8)

    def ffn(h):
        for o in range(4):
            gather[h].column(o)
        rows = tok[h].reshape(256, width)
        hidden = []
        for k in range(2):
            pre = jnp.dot(rows, w1[k], preferred_element_type=F32)
            hidden.append((pre * 0.5 * (1.0 + lax.erf(pre * 0.7071067811865476))).astype(BF16))
        out = jnp.dot(hidden[0], w2[0], preferred_element_type=F32)
        out = out + jnp.dot(hidden[1], w2[1], preferred_element_type=F32)
        part[h] = out.astype(BF16).reshape(16, 16, width)

    def first_stage(h):
        for o in ORDER + (0,):
            for d in ORDER:
                vd = (v + d) % 4
                send(
                    part.at[h, ((u + o) % 4) * 4 + vd], r1.at[h, 3 - d, o],
                    rs_out.at[h, 0], r1_recv.at[h, o], at(u, vd),
                )

    def second_stage(h, o):
        uo = (u + o) % 4
        arrived(r1.at[h, :, o], r1_recv.at[h, o])
        total = part[h, uo * 4 + v].astype(F32)
        for k in range(3):
            total = total + r1[h, k, o].astype(F32)
        s1[h, o] = total.astype(BF16)
        send(s1.at[h, o], r2.at[h, 3 - o], rs_out.at[h, 1], r2_recv.at[h], at(uo, v))

    def embed(h):
        total = part[h, me].astype(F32)
        arrived(r1.at[h, :, 0], r1_recv.at[h, 0])
        for k in range(3):
            total = total + r1[h, k, 0].astype(F32)
        arrived(r2.at[h], r2_recv.at[h])
        for k in range(3):
            total = total + r2[h, k].astype(F32)
        stream = xv[pl.ds(h * 16, 16), :].astype(F32) + total
        pooled = layer_norm(stream, g2v[...][None, :]).astype(BF16)
        projected = jnp.dot(pooled, mapv[...], preferred_element_type=F32)
        emb[h, me] = (
            projected * lax.rsqrt(jnp.sum(projected * projected, axis=-1, keepdims=True) + 1e-06)
        ).astype(BF16)

    spread = [PlaneGather(u, v, at, emb.at[h], (e_1.at[h], e_2.at[h], e_3.at[h], e_out.at[h]), ()) for h in range(2)]

    sharp = sharp_ref[0]

    def logits(h):
        for o in range(4):
            spread[h].column(o)
        rows = emb[h].reshape(256, edim)
        vals = []
        for core in (1 - c, c):
            classes = cls[core].reshape(512, edim)
            val = sharp * lax.dot_general(rows, classes, (((1,), (1,)), ((), ())), preferred_element_type=F32)
            for j in range(16):
                uu, vv = j // 4, j % 4
                place = (uu + c * (vv - uu)) * 4 + vv + c * (uu - vv)
                piece = val[j * 16 : (j + 1) * 16]
                if vals:
                    lg[place, c, h] = piece
                else:
                    stage[h, j] = piece
                    send(stage.at[h, j], lg.at[place, c, h], lg_out, lg_recv, mate)
            vals.append(val)
        top = jnp.maximum(jnp.max(vals[0], axis=-1, keepdims=True), jnp.max(vals[1], axis=-1, keepdims=True))
        total = jnp.sum(jnp.exp(vals[0] - top) + jnp.exp(vals[1] - top), axis=-1, keepdims=True)
        lse = top + jnp.log(total)
        for q in range(2):
            half = jnp.broadcast_to(lse[q * 128 : (q + 1) * 128], (128, 128)).T
            lse_x[0, h * 2 + q : h * 2 + q + 1, :] = half[0:1, :]

    gather[0].start()
    first_sums()
    z_reduce(0)
    group_sums(3)
    gather[1].start()
    send(w1_hbm, w1.at[c], w_send.at[0], w_recv.at[0], mate)
    send(w2_hbm, w2.at[c], w_send.at[1], w_recv.at[1], mate)
    group_sums(6)
    gather[0].forward(1)
    gather[0].forward(0)
    gather[0].forward(3)
    group_sums(5)
    gather[0].forward(2)
    z_reduce(1)
    group_sums(0)
    gather[1].forward(3)
    gather[1].forward(0)
    group_sums(7)
    group_sums(2)
    gather[1].forward(2)
    gather[1].forward(1)
    group_sums(1)
    z_reduce(2)
    for i in (4, 5, 6, 7):
        loads[i].wait()
    arrived(w1.at[1 - c], w_recv.at[0])
    arrived(w2.at[1 - c], w_recv.at[1])
    ffn(0)
    first_stage(0)
    z_reduce(3)
    ffn(1)
    first_stage(1)
    z_total()
    z_gather(0)
    second_stage(0, 2)
    second_stage(0, 1)
    second_stage(1, 1)
    second_stage(0, 3)
    second_stage(1, 3)
    z_gather(1)
    second_stage(1, 2)
    embed(0)
    spread[0].start()
    spread[0].forward(0)
    z_gather(2)
    spread[0].forward(1)
    spread[0].forward(3)
    embed(1)
    spread[1].start()
    spread[0].forward(2)
    spread[1].forward(0)
    z_gather(3)
    spread[1].forward(1)
    spread[1].forward(3)
    z_gather(4)
    spread[1].forward(2)
    arrived(cls.at[1 - c], pair_recv)
    logits(0)
    logits(1)

    def merge(values):
        top = values[0]
        for v in values[1:]:
            top = jnp.maximum(top, v)
        acc = jnp.exp(values[0] - top)
        for v in values[1:]:
            acc = acc + jnp.exp(v - top)
        return top + jnp.log(acc)

    for i, d in enumerate(ORDER):
        send(lse_x.at[0], lse_x.at[4 - d], l_out.at[0], lx_recv.at[4 - d], x_peers[i])
    for d in ORDER:
        arrived(lse_x.at[d], lx_recv.at[d])
    lse_y[c, 0] = merge([lse_x[i] for i in range(4)])
    mine = lse_y.at[c, 0]
    for i, d in enumerate(ORDER):
        send(mine, lse_y.at[c, 4 - d], l_out.at[1], ly_recv.at[c, 4 - d], y_peers[i])
        send(mine, lse_y.at[c, 4 - d], l_out.at[1], ly_recv.at[c, 4 - d], y_others[i])
    send(mine, mine, l_out.at[1], ly_recv.at[c, 0], mate)

    for h in range(2):
        gather[h].finish()
        spread[h].finish()
        arrived(part.at[h, pl.ds(0, 12)], rs_out.at[h, 0])
        arrived(r2.at[h], rs_out.at[h, 1])
    arrived(w1.at[c], w_send.at[0])
    arrived(w2.at[c], w_send.at[1])
    arrived(gs.at[pl.ds(0, 7)], z_out)
    arrived(gs.at[pl.ds(0, 7)], za_out)
    arrived(cls.at[c], pair_out)
    arrived(stage, lg_out)
    arrived(lse_x.at[pl.ds(0, 3)], l_out.at[0])
    arrived(lg.at[:, 1 - c], lg_recv)

    arrived(lse_y.at[1 - c, 0], ly_recv.at[1 - c, 0])
    for d in ORDER:
        for core in (c, 1 - c):
            arrived(lse_y.at[core, d], ly_recv.at[core, d])
    for core in range(2):
        lse = merge([lse_y[core, i] for i in range(4)])
        for row in range(4):
            columns = jnp.broadcast_to(lse[row : row + 1, :], (128, 128)).T
            for k in range(8):
                j = (row % 2) * 8 + k
                place = (j % 4) * 4 + j // 4 if core else j
                lse_out[place, core, row // 2] = columns[k * 16 : (k + 1) * 16]
    arrived(lse_y.at[0, pl.ds(0, 3)], l_out.at[1])
    arrived(lse_y.at[0], l_out.at[1])


def shards(states, gain1, w1, w2, gain2, mapper, prompts, multiplicity, sharpness):
    width = states.shape[1]
    edim = mapper.shape[1]
    hbm = pl.BlockSpec(memory_space=pltpu.HBM)
    vmem = pl.BlockSpec(memory_space=pltpu.VMEM)
    dma = pltpu.SemaphoreType.DMA
    logit, lse = pl.pallas_call(
        kernel,
        name="whole",
        out_shape=(pltpu.VMEM((16, 2, 2, 16, 512), F32), pltpu.VMEM((16, 2, 2, 16, 128), F32)),
        in_specs=[hbm] * 8 + [pl.BlockSpec(memory_space=pltpu.SMEM)],
        out_specs=(vmem, vmem),
        scratch_shapes=[
            pltpu.VMEM((32, width), BF16),
            pltpu.VMEM((width,), F32),
            pltpu.VMEM((width,), F32),
            pltpu.VMEM((16, 512), jnp.int32),
            pltpu.VMEM((2, 16, 16, width), BF16),
            pltpu.VMEM((2, width, 256), BF16),
            pltpu.VMEM((2, 256, width), BF16),
            pltpu.VMEM((2, 16, 16, width), BF16),
            pltpu.VMEM((2, 3, 4, 16, width), BF16),
            pltpu.VMEM((2, 4, 16, width), BF16),
            pltpu.VMEM((2, 3, 16, width), BF16),
            pltpu.VMEM((width, edim), BF16),
            pltpu.VMEM((2, 16, 16, edim), BF16),
            pltpu.VMEM((512, 2, edim), BF16),
            pltpu.VMEM((2, 512, 128), F32),
            pltpu.VMEM((8, 64, edim), BF16),
            pltpu.VMEM((2, 4, 64, edim), BF16),
            pltpu.VMEM((2, 4, 64, edim), BF16),
            pltpu.VMEM((2, 8, 64, edim), BF16),
            pltpu.VMEM((2, 16, 16, 512), F32),
            pltpu.VMEM((4, 4, 128), F32),
            pltpu.VMEM((2, 4, 4, 128), F32),
            dma((8,)), dma((2,)), dma((2,)),
            dma((2, 4)), dma((2, 4, 2)), dma((2, 4)), dma((2,)),
            dma((2, 4)), dma((2, 4, 2)), dma((2, 4)), dma((2,)),
            dma((2, 4)), dma((2,)), dma((2, 2)),
            dma((2, 2, 4)), dma(()), dma((2, 2, 4)), dma(()),
            dma(()), dma(()), dma(()), dma(()),
            dma((4,)), dma((2, 4)), dma((2,)),
        ],
        compiler_params=pltpu.CompilerParams(
            collective_id=0, has_side_effects=True, vmem_limit_bytes=61 * 1024 * 1024
        ),
    )(states, gain1, w1, w2, gain2, mapper, prompts, multiplicity.T, sharpness)
    return logit.reshape(1024, 512) - lse.reshape(1024, 128)[:, :1]


def solution(mesh):
    in_specs = (
        P(("img", "cls"), None),
        P(),
        P(None, "cls"),
        P("cls", None),
        P(),
        P(),
        P("cls", "img", None),
        P("cls", None),
        P(),
    )
    out_specs = P("img", "cls")
    return jax.shard_map(shards, mesh=mesh, in_specs=in_specs, out_specs=out_specs, check_vma=False)
```

```python
import jax
import jax.numpy as jnp
from jax import lax
from jax.experimental import pallas as pl
from jax.experimental.pallas import tpu as pltpu
from jax.sharding import PartitionSpec as P

MESH = pl.DeviceIdType.MESH
F32 = jnp.float32
BF16 = jnp.bfloat16
ORDER = (1, 3, 2)


def layer_norm(values, gain):
    center = values - jnp.mean(values, axis=-1, keepdims=True)
    variance = jnp.mean(center * center, axis=-1, keepdims=True)
    return center * lax.rsqrt(variance + 1e-05) * gain


def arrived(ref, sem):
    pltpu.make_async_copy(ref, ref, sem).wait()


class PlaneGather:
    def __init__(self, u, v, at, buf, sems, relayed):
        self.u, self.v, self.at, self.buf, self.relayed = u, v, at, buf, relayed
        self.first, self.second, self.third, self.out = sems

    def send(self, uu, vv, to, sem):
        piece = self.buf.at[uu * 4 + vv]
        pltpu.make_async_remote_copy(
            src_ref=piece, dst_ref=piece, send_sem=self.out, recv_sem=sem, device_id=to, device_id_type=MESH
        ).start()

    def start(self):
        for d in ORDER:
            self.send(self.u, self.v, self.at((self.u + d) % 4, self.v), self.first.at[4 - d])

    def forward(self, o):
        u, v = self.u, self.v
        uo = (u + o) % 4
        if o:
            arrived(self.buf.at[uo * 4 + v], self.first.at[o])
        self.send(uo, v, self.at(u, (v + 1) % 4), self.second.at[o, 0])
        self.send(uo, v, self.at(u, (v + 3) % 4), self.second.at[o, 1])
        if o not in self.relayed:
            self.send(uo, v, self.at(u, (v + 2) % 4), self.third.at[o])

    def relay(self, o):
        u, v = self.u, self.v
        came, to = (3, 1) if o % 2 == 0 else (1, 3)
        uo, vs = (u + o) % 4, (v + came) % 4
        arrived(self.buf.at[uo * 4 + vs], self.second.at[o, o % 2])
        self.send(uo, vs, self.at(u, (v + to) % 4), self.third.at[o])

    def column(self, o):
        uo = (self.u + o) % 4
        for side, d in ((0, 3), (1, 1)):
            if o not in self.relayed or side != o % 2:
                arrived(self.buf.at[uo * 4 + (self.v + d) % 4], self.second.at[o, side])
        arrived(self.buf.at[uo * 4 + (self.v + 2) % 4], self.third.at[o])

    def finish(self):
        arrived(self.buf.at[pl.ds(0, 15)], self.out)


def kernel(
    x_hbm, g1_hbm, w1_hbm, w2_hbm, g2_hbm, map_hbm, tpl_hbm, mult_hbm, sharp_ref,
    lg, lse_out,
    xv, g1v, g2v, multv, tok, w1, w2, part, r1, s1, r2, mapv, emb, tplv, shc, gs, zr, zs, cls,
    stage, lse_x, lse_y,
    load_sem, w_send, w_recv, g_1, g_2, g_3, g_out, e_1, e_2, e_3, e_out,
    r1_recv, r2_recv, rs_out, z_recv, z_out, za_recv, za_out, pair_recv, pair_out, lg_recv, lg_out, lx_recv, ly_recv, l_out,
):
    m = lax.axis_index("cls")
    z = lax.axis_index("img")
    x, y, c = m // 8, (m // 2) % 4, m % 2
    u, v = x + c * (y - x), y + c * (x - y)
    me = u * 4 + v
    width, edim = tok.shape[-1], emb.shape[-1]

    def device(xx, yy, cc):
        return (z, (xx * 4 + yy) * 2 + cc)

    def at(uu, vv):
        return device(uu + c * (vv - uu), vv + c * (uu - vv), c)

    mate = device(x, y, 1 - c)
    z_up, z_down = ((z + 1) % 8, m), ((z + 7) % 8, m)

    def send(src, dst, s_sem, r_sem, to):
        pltpu.make_async_remote_copy(
            src_ref=src, dst_ref=dst, send_sem=s_sem, recv_sem=r_sem, device_id=to, device_id_type=MESH
        ).start()

    barrier = pltpu.get_barrier_semaphore()
    x_peers = [device((x + d) % 4, y, c) for d in ORDER]
    y_peers = [device(x, (y + d) % 4, c) for d in ORDER]
    y_others = [device(x, (y + d) % 4, 1 - c) for d in ORDER]
    partners = x_peers + y_peers + [mate, z_up, z_down] + y_others
    loads = [
        pltpu.make_async_copy(src, dst, load_sem.at[i])
        for i, (src, dst) in enumerate(
            (
                (x_hbm, xv), (g1_hbm, g1v), (mult_hbm, multv), (tpl_hbm, tplv),
                (w1_hbm, w1.at[c]), (w2_hbm, w2.at[c]), (g2_hbm, g2v), (map_hbm, mapv),
            )
        )
    ]
    loads[0].start()
    loads[1].start()
    for to in partners:
        pl.semaphore_signal(barrier, inc=1, device_id=to, device_id_type=MESH)
    for load in loads[2:]:
        load.start()

    loads[0].wait()
    loads[1].wait()
    states = xv[...].astype(F32)
    normed = layer_norm(states, g1v[...][None, :]).astype(BF16)
    tok[0, me] = normed[:16]
    tok[1, me] = normed[16:]

    def group_sums(*offsets):
        for off in offsets:
            k = (z + off) % 8

            @pl.loop(0, 2)
            def _(i):
                rows = pl.ds(k * 64 + i * 32, 32)
                acc = None
                for t in range(2):
                    tmpl = tplv[rows, t, :].astype(F32)
                    coef = shc[t, rows, 0:1] * lax.rsqrt(jnp.sum(tmpl * tmpl, axis=-1, keepdims=True) + 1e-06)
                    acc = coef * tmpl if acc is None else acc + coef * tmpl
                gs[k, pl.ds(i * 32, 32), :] = acc.astype(BF16)

    pl.semaphore_wait(barrier, len(partners))

    gather = [PlaneGather(u, v, at, tok.at[h], (g_1.at[h], g_2.at[h], g_3.at[h], g_out.at[h]), ()) for h in range(2)]
    def first_sums():
        loads[2].wait()
        weights = multv[...].astype(F32)
        total = jnp.sum(weights, axis=0, keepdims=True)
        row_id = lax.broadcasted_iota(jnp.int32, weights.shape, 0)
        for t in range(2):
            own = jnp.sum(jnp.where(row_id == 2 * z + t, weights, 0.0), axis=0, keepdims=True)
            portion = own / total
            for q in range(4):
                shc[t, pl.ds(q * 128, 128), :] = jnp.broadcast_to(portion[:, q * 128 : (q + 1) * 128], (128, 128)).T
        loads[3].wait()
        group_sums(4)

    halves = (pl.ds(0, 640), pl.ds(640, 640))

    def z_reduce(s):
        for way, half in ((0, 0), (1, 1), (0, 1), (1, 0)):
            if s == 0 and way != half:
                continue
            cols = halves[half]
            k = (z + 4 + s) % 8 if way == 0 else (z + 4 - s + 8) % 8
            first = s == 0 or (s == 1 and way != half)
            if first:
                src = gs.at[k, :, cols]
            else:
                came = zr.at[way, s - 1, :, cols]
                arrived(came, z_recv.at[way, half, s - 1])
                zs[way, s, :, cols] = (gs[k, :, cols].astype(F32) + came[...].astype(F32)).astype(BF16)
                src = zs.at[way, s, :, cols]
            send(src, zr.at[way, s, :, cols], z_out, z_recv.at[way, half, s], z_down if way == 0 else z_up)

    def to_mate(k):
        send(cls.at[c, k], cls.at[c, k], pair_out, pair_recv, mate)

    def z_total():
        for half in range(2):
            cols = halves[half]
            for way in range(2):
                arrived(zr.at[way, 3, :, cols], z_recv.at[way, half, 3])
            cls[c, z, :, cols] = (
                gs[z, :, cols].astype(F32) + zr[0, 3, :, cols].astype(F32) + zr[1, 3, :, cols].astype(F32)
            ).astype(BF16)

    def z_gather(s):
        for way, half in ((0, 0), (1, 1), (0, 1), (1, 0)):
            cols = halves[half]
            far = 4 if way == half else 3
            k = (z + s) % 8 if way == 0 else (z - s + 8) % 8
            if s > far:
                continue
            chunk = cls.at[c, k, :, cols]
            if s > 0:
                arrived(chunk, za_recv.at[way, half, s - 1])
            if s < far:
                send(chunk, chunk, za_out, za_recv.at[way, half, s], z_down if way == 0 else z_up)
        for k in {0: (0,), 4: (4,)}.get(s, (s, 8 - s)):
            to_mate((z + k) % 8)

    def ffn(h):
        for o in range(4):
            gather[h].column(o)
        rows = tok[h].reshape(256, width)
        hidden = []
        for k in range(2):
            pre = jnp.dot(rows, w1[k], preferred_element_type=F32)
            hidden.append((pre * 0.5 * (1.0 + lax.erf(pre * 0.7071067811865476))).astype(BF16))
        out = jnp.dot(hidden[0], w2[0], preferred_element_type=F32)
        out = out + jnp.dot(hidden[1], w2[1], preferred_element_type=F32)
        part[h] = out.astype(BF16).reshape(16, 16, width)

    def first_stage(h):
        for o in ORDER + (0,):
            for d in ORDER:
                vd = (v + d) % 4
                send(
                    part.at[h, ((u + o) % 4) * 4 + vd], r1.at[h, 3 - d, o],
                    rs_out.at[h, 0], r1_recv.at[h, o], at(u, vd),
                )

    def second_stage(h, o):
        uo = (u + o) % 4
        arrived(r1.at[h, :, o], r1_recv.at[h, o])
        total = part[h, uo * 4 + v].astype(F32)
        for k in range(3):
            total = total + r1[h, k, o].astype(F32)
        s1[h, o] = total.astype(BF16)
        send(s1.at[h, o], r2.at[h, 3 - o], rs_out.at[h, 1], r2_recv.at[h], at(uo, v))

    def embed(h):
        total = part[h, me].astype(F32)
        arrived(r1.at[h, :, 0], r1_recv.at[h, 0])
        for k in range(3):
            total = total + r1[h, k, 0].astype(F32)
        arrived(r2.at[h], r2_recv.at[h])
        for k in range(3):
            total = total + r2[h, k].astype(F32)
        stream = xv[pl.ds(h * 16, 16), :].astype(F32) + total
        pooled = layer_norm(stream, g2v[...][None, :]).astype(BF16)
        projected = jnp.dot(pooled, mapv[...], preferred_element_type=F32)
        emb[h, me] = (
            projected * lax.rsqrt(jnp.sum(projected * projected, axis=-1, keepdims=True) + 1e-06)
        ).astype(BF16)

    spread = [PlaneGather(u, v, at, emb.at[h], (e_1.at[h], e_2.at[h], e_3.at[h], e_out.at[h]), ()) for h in range(2)]

    sharp = sharp_ref[0]

    def logits(h):
        for o in range(4):
            spread[h].column(o)
        rows = emb[h].reshape(256, edim)
        vals = []
        for core in (1 - c, c):
            classes = cls[core].reshape(512, edim)
            val = sharp * lax.dot_general(rows, classes, (((1,), (1,)), ((), ())), preferred_element_type=F32)
            for j in range(16):
                uu, vv = j // 4, j % 4
                place = (uu + c * (vv - uu)) * 4 + vv + c * (uu - vv)
                piece = val[j * 16 : (j + 1) * 16]
                if vals:
                    lg[place, c, h] = piece
                else:
                    stage[h, j] = piece
                    send(stage.at[h, j], lg.at[place, c, h], lg_out, lg_recv, mate)
            vals.append(val)
        top = jnp.maximum(jnp.max(vals[0], axis=-1, keepdims=True), jnp.max(vals[1], axis=-1, keepdims=True))
        total = jnp.sum(jnp.exp(vals[0] - top) + jnp.exp(vals[1] - top), axis=-1, keepdims=True)
        lse = top + jnp.log(total)
        for q in range(2):
            half = jnp.broadcast_to(lse[q * 128 : (q + 1) * 128], (128, 128)).T
            lse_x[0, h * 2 + q : h * 2 + q + 1, :] = half[0:1, :]

    gather[0].start()
    first_sums()
    z_reduce(0)
    send(w1_hbm, w1.at[c], w_send.at[0], w_recv.at[0], mate)
    send(w2_hbm, w2.at[c], w_send.at[1], w_recv.at[1], mate)
    group_sums(2)
    gather[0].forward(0)
    group_sums(5)
    group_sums(7)
    gather[1].start()
    gather[0].forward(1)
    group_sums(3)
    z_reduce(1)
    gather[0].forward(2)
    gather[0].forward(3)
    group_sums(1)
    group_sums(6)
    gather[1].forward(0)
    gather[1].forward(3)
    gather[1].forward(2)
    gather[1].forward(1)
    group_sums(0)
    z_reduce(2)
    for i in (4, 5, 6, 7):
        loads[i].wait()
    arrived(w1.at[1 - c], w_recv.at[0])
    arrived(w2.at[1 - c], w_recv.at[1])
    ffn(0)
    first_stage(0)
    z_reduce(3)
    ffn(1)
    first_stage(1)
    z_total()
    z_gather(0)
    second_stage(0, 2)
    second_stage(0, 3)
    second_stage(0, 1)
    z_gather(1)
    second_stage(1, 2)
    second_stage(1, 1)
    second_stage(1, 3)
    embed(0)
    spread[0].start()
    spread[0].forward(0)
    z_gather(2)
    embed(1)
    spread[1].start()
    spread[1].forward(0)
    spread[0].forward(2)
    spread[0].forward(1)
    z_gather(3)
    spread[0].forward(3)
    spread[1].forward(2)
    spread[1].forward(3)
    z_gather(4)
    spread[1].forward(1)
    arrived(cls.at[1 - c], pair_recv)
    logits(0)
    logits(1)

    def merge(values):
        top = values[0]
        for v in values[1:]:
            top = jnp.maximum(top, v)
        acc = jnp.exp(values[0] - top)
        for v in values[1:]:
            acc = acc + jnp.exp(v - top)
        return top + jnp.log(acc)

    for i, d in enumerate(ORDER):
        send(lse_x.at[0], lse_x.at[4 - d], l_out.at[0], lx_recv.at[4 - d], x_peers[i])
    for d in ORDER:
        arrived(lse_x.at[d], lx_recv.at[d])
    lse_y[c, 0] = merge([lse_x[i] for i in range(4)])
    mine = lse_y.at[c, 0]
    for i, d in enumerate(ORDER):
        send(mine, lse_y.at[c, 4 - d], l_out.at[1], ly_recv.at[c, 4 - d], y_peers[i])
        send(mine, lse_y.at[c, 4 - d], l_out.at[1], ly_recv.at[c, 4 - d], y_others[i])
    send(mine, mine, l_out.at[1], ly_recv.at[c, 0], mate)

    for h in range(2):
        gather[h].finish()
        spread[h].finish()
        arrived(part.at[h, pl.ds(0, 12)], rs_out.at[h, 0])
        arrived(r2.at[h], rs_out.at[h, 1])
    arrived(w1.at[c], w_send.at[0])
    arrived(w2.at[c], w_send.at[1])
    arrived(gs.at[pl.ds(0, 7)], z_out)
    arrived(gs.at[pl.ds(0, 7)], za_out)
    arrived(cls.at[c], pair_out)
    arrived(stage, lg_out)
    arrived(lse_x.at[pl.ds(0, 3)], l_out.at[0])
    arrived(lg.at[:, 1 - c], lg_recv)

    arrived(lse_y.at[1 - c, 0], ly_recv.at[1 - c, 0])
    for d in ORDER:
        for core in (c, 1 - c):
            arrived(lse_y.at[core, d], ly_recv.at[core, d])
    for core in range(2):
        lse = merge([lse_y[core, i] for i in range(4)])
        for row in range(4):
            columns = jnp.broadcast_to(lse[row : row + 1, :], (128, 128)).T
            for k in range(8):
                j = (row % 2) * 8 + k
                place = (j % 4) * 4 + j // 4 if core else j
                lse_out[place, core, row // 2] = columns[k * 16 : (k + 1) * 16]
    arrived(lse_y.at[0, pl.ds(0, 3)], l_out.at[1])
    arrived(lse_y.at[0], l_out.at[1])


def shards(states, gain1, w1, w2, gain2, mapper, prompts, multiplicity, sharpness):
    width = states.shape[1]
    edim = mapper.shape[1]
    hbm = pl.BlockSpec(memory_space=pltpu.HBM)
    vmem = pl.BlockSpec(memory_space=pltpu.VMEM)
    dma = pltpu.SemaphoreType.DMA
    logit, lse = pl.pallas_call(
        kernel,
        name="whole",
        out_shape=(pltpu.VMEM((16, 2, 2, 16, 512), F32), pltpu.VMEM((16, 2, 2, 16, 128), F32)),
        in_specs=[hbm] * 8 + [pl.BlockSpec(memory_space=pltpu.SMEM)],
        out_specs=(vmem, vmem),
        scratch_shapes=[
            pltpu.VMEM((32, width), BF16),
            pltpu.VMEM((width,), F32),
            pltpu.VMEM((width,), F32),
            pltpu.VMEM((16, 512), jnp.int32),
            pltpu.VMEM((2, 16, 16, width), BF16),
            pltpu.VMEM((2, width, 256), BF16),
            pltpu.VMEM((2, 256, width), BF16),
            pltpu.VMEM((2, 16, 16, width), BF16),
            pltpu.VMEM((2, 3, 4, 16, width), BF16),
            pltpu.VMEM((2, 4, 16, width), BF16),
            pltpu.VMEM((2, 3, 16, width), BF16),
            pltpu.VMEM((width, edim), BF16),
            pltpu.VMEM((2, 16, 16, edim), BF16),
            pltpu.VMEM((512, 2, edim), BF16),
            pltpu.VMEM((2, 512, 128), F32),
            pltpu.VMEM((8, 64, edim), BF16),
            pltpu.VMEM((2, 4, 64, edim), BF16),
            pltpu.VMEM((2, 4, 64, edim), BF16),
            pltpu.VMEM((2, 8, 64, edim), BF16),
            pltpu.VMEM((2, 16, 16, 512), F32),
            pltpu.VMEM((4, 4, 128), F32),
            pltpu.VMEM((2, 4, 4, 128), F32),
            dma((8,)), dma((2,)), dma((2,)),
            dma((2, 4)), dma((2, 4, 2)), dma((2, 4)), dma((2,)),
            dma((2, 4)), dma((2, 4, 2)), dma((2, 4)), dma((2,)),
            dma((2, 4)), dma((2,)), dma((2, 2)),
            dma((2, 2, 4)), dma(()), dma((2, 2, 4)), dma(()),
            dma(()), dma(()), dma(()), dma(()),
            dma((4,)), dma((2, 4)), dma((2,)),
        ],
        compiler_params=pltpu.CompilerParams(
            collective_id=0, has_side_effects=True, vmem_limit_bytes=61 * 1024 * 1024
        ),
    )(states, gain1, w1, w2, gain2, mapper, prompts, multiplicity.T, sharpness)
    return logit.reshape(1024, 512) - lse.reshape(1024, 128)[:, :1]


def solution(mesh):
    in_specs = (
        P(("img", "cls"), None),
        P(),
        P(None, "cls"),
        P("cls", None),
        P(),
        P(),
        P("cls", "img", None),
        P("cls", None),
        P(),
    )
    out_specs = P("img", "cls")
    return jax.shard_map(shards, mesh=mesh, in_specs=in_specs, out_specs=out_specs, check_vma=False)
```
